256 devices in a mesh: dp: 64 (over x, z, core), mp: 4 (over y).
Axes of the slice: x: 4, y: 4, z: 8, core: 2. Of those that a mesh axis runs over, the one named last changes fastest.
Arguments:
- gradient: bfloat16 [128, 1024, 1024], P('dp', 'mp'), may hold values from -3 to 3
- left_codes: bfloat16 [128, 1024, 1024], P('dp', 'mp'), may hold values from -1 to 1
- left_scales: bfloat16 [128, 1024], P('dp', 'mp'), may hold values from 0.5 to 5
- right_codes: bfloat16 [128, 1024, 1024], P('dp', 'mp'), may hold values from -1 to 1
- right_scales: bfloat16 [128, 1024], P('dp', 'mp'), may hold values from 0.5 to 5
- left_root_codes: bfloat16 [128, 1024, 1024], P('dp', 'mp'), may hold values from -0.1 to 1, as said below
- left_root_scales: bfloat16 [128, 1024], P('dp', 'mp'), may hold values from 0.5 to 2
- right_root_codes: bfloat16 [128, 1024, 1024], P('dp', 'mp'), may hold values from -0.1 to 1, as said below
- right_root_scales: bfloat16 [128, 1024], P('dp', 'mp'), may hold values from 0.5 to 2
- owner_plan: int32 [128], replicated, may hold values from 0 to 127, as said below
Outputs:
- new_left_codes: bfloat16 [128, 1024, 1024], P('dp', 'mp')
- new_left_scales: bfloat16 [128, 1024], P('dp', 'mp')
- new_right_codes: bfloat16 [128, 1024, 1024], P('dp', 'mp')
- new_right_scales: bfloat16 [128, 1024], P('dp', 'mp')
- update: bfloat16 [128, 1024, 1024], P('dp', 'mp')
The draws below stay inside these ranges and needn't reach their ends.
Inputs may be any that keep to these rules, and one draw needn't show every extreme that they name: `left_root_codes`: each row i has one entry on the diagonal between 0.6 and 1 and small entries elsewhere. `right_root_codes`: each row i has one entry on the diagonal between 0.6 and 1 and small entries elsewhere. `owner_plan`: A permutation of the 128 slots; slot s lies on device s // 2 of dp. Exactly 12 blocks get a slot on another device; from each device at most one block leaves and at most one arrives, and an arriving block takes the slot that the device's leaving block frees; every other block keeps its slot.
All inputs are finite; a program needn't handle non-finite values. Where the reference program divides by a largest or mean magnitude, that divisor is 1e-20 or more.
Results may differ from the reference program's by a relative error of at most 0.009.
Values may be sent and summed in bfloat16 or wider, within the bound.
A program may use at most 64 MiB of HBM per device.

```python
import math
import jax
import jax.numpy as jnp
from jax import lax

BLK = 1024
SLOTS = 2
BLOCKS = 128
MOVED = 12


def draw_gradient(key, part):
    base = jax.random.fold_in(key, 3)
    first, second, third = jax.random.split(base, 3)
    row_scale = jnp.exp(jax.random.uniform(first, (BLOCKS, BLK, 1), jnp.float32, math.log(0.3), math.log(3.0)))
    col_scale = jnp.exp(jax.random.uniform(second, (BLOCKS, 1, BLK), jnp.float32, math.log(0.3), math.log(3.0)))
    values = jax.random.normal(third, (BLOCKS, BLK, BLK)) * row_scale * col_scale
    values = values / math.sqrt(BLK)
    return jnp.clip(values, -3.0, 3.0).astype(jnp.bfloat16)


def root_codes(key):
    first, second = jax.random.split(key)
    diagonal = jax.random.uniform(first, (BLOCKS, BLK, 1), jnp.float32, 0.6, 1.0)
    spread = jnp.clip(0.02 * jax.random.normal(second, (BLOCKS, BLK, BLK)), -0.09, 0.09)
    identity = jnp.eye(BLK, dtype=jnp.float32)[None]
    return (spread * (1.0 - identity) + identity * diagonal).astype(jnp.bfloat16)


def draw_left_root_codes(key, part):
    return root_codes(jax.random.fold_in(key, 11))


def draw_right_root_codes(key, part):
    return root_codes(jax.random.fold_in(key, 12))


def draw_owner_plan(key, part):
    base = jax.random.fold_in(key, 5)
    owners = BLOCKS // SLOTS
    picked = jax.random.permutation(jax.random.fold_in(base, 1), owners)[:MOVED]
    sides = jax.random.randint(jax.random.fold_in(base, 2), (MOVED,), 0, SLOTS)
    sources = (picked * SLOTS + sides).astype(jnp.int32)
    targets = jnp.roll(sources, -1)
    return jnp.arange(BLOCKS, dtype=jnp.int32).at[sources].set(targets)


def shard_levels(stream_key, dims, cuts, least, largest):
    def one(position, parts):
        steps = jax.random.uniform(jax.random.fold_in(jax.random.fold_in(stream_key, 6), position), (parts,), jnp.float32, least / len(cuts), largest / len(cuts))
        return jnp.repeat(jnp.exp(steps), dims[position] // parts).reshape((-1,) + (1,) * (len(dims) - position - 1))

    level = one(*cuts[0])
    for cut in cuts[1:]:
        level = level * one(*cut)
    return level


def setup_inputs(seed: int = 0) -> dict:
    seeds = jax.random.split(jax.random.key(seed), 11)
    return {
        "gradient": draw_gradient(jax.random.fold_in(seeds[10], 71), 0),
        "left_codes": jnp.clip(jax.random.uniform(seeds[1], (BLOCKS, BLK, BLK), jnp.float32, -1.0, 1.0) * shard_levels(seeds[1], (BLOCKS, BLK, BLK), ((0, 64), (1, 4)), -0.4, 0.0), -1.0, 1.0).astype(jnp.bfloat16),
        "left_scales": jnp.clip(jnp.exp(math.log(5.0) - 2.3025851 * jax.random.uniform(seeds[2], (BLOCKS, BLK), jnp.float32) ** shard_levels(seeds[2], (BLOCKS, BLK), ((0, 64), (1, 4)), -0.2, 0.2)), 0.5, 5.0).astype(jnp.bfloat16),
        "right_codes": jnp.clip(jax.random.uniform(seeds[3], (BLOCKS, BLK, BLK), jnp.float32, -1.0, 1.0) * shard_levels(seeds[3], (BLOCKS, BLK, BLK), ((0, 64), (1, 4)), -0.4, 0.0), -1.0, 1.0).astype(jnp.bfloat16),
        "right_scales": jnp.clip(jnp.exp(math.log(5.0) - 2.3025851 * jax.random.uniform(seeds[4], (BLOCKS, BLK), jnp.float32) ** shard_levels(seeds[4], (BLOCKS, BLK), ((0, 64), (1, 4)), -0.2, 0.2)), 0.5, 5.0).astype(jnp.bfloat16),
        "left_root_codes": draw_left_root_codes(jax.random.fold_in(seeds[10], 71), 0),
        "left_root_scales": jnp.clip(jnp.exp(math.log(2.0) - 1.3862944 * jax.random.uniform(seeds[6], (BLOCKS, BLK), jnp.float32) ** shard_levels(seeds[6], (BLOCKS, BLK), ((0, 64), (1, 4)), -0.2, 0.2)), 0.5, 2.0).astype(jnp.bfloat16),
        "right_root_codes": draw_right_root_codes(jax.random.fold_in(seeds[10], 71), 0),
        "right_root_scales": jnp.clip(jnp.exp(math.log(2.0) - 1.3862944 * jax.random.uniform(seeds[8], (BLOCKS, BLK), jnp.float32) ** shard_levels(seeds[8], (BLOCKS, BLK), ((0, 64), (1, 4)), -0.2, 0.2)), 0.5, 2.0).astype(jnp.bfloat16),
        "owner_plan": draw_owner_plan(jax.random.fold_in(seeds[10], 71), 0),
    }


DECAY = 0.95
EPSILON = 1e-06

def dequantize(codes, scales):
    return codes.astype(jnp.float32) * scales.astype(jnp.float32)[:, None]

def requantize(matrix):
    scales = (lax.optimization_barrier(jnp.max(jnp.abs(matrix), axis=-1)) + EPSILON).astype(jnp.bfloat16)
    codes = (matrix / scales.astype(jnp.float32)[:, None]).astype(jnp.bfloat16)
    return (codes, scales)

def one_block(entries):
    grad_block, left_c, left_s, right_c, right_s, lroot_c, lroot_s, rroot_c, rroot_s = entries
    left_new = DECAY * dequantize(left_c, left_s) + jnp.dot(grad_block, grad_block.T, preferred_element_type=jnp.float32)
    right_new = DECAY * dequantize(right_c, right_s) + jnp.dot(grad_block.T, grad_block, preferred_element_type=jnp.float32)
    left_root = dequantize(lroot_c, lroot_s).astype(jnp.bfloat16)
    right_root = dequantize(rroot_c, rroot_s).astype(jnp.bfloat16)
    lifted = jnp.dot(left_root, grad_block, preferred_element_type=jnp.float32).astype(jnp.bfloat16)
    direction = jnp.dot(lifted, right_root, preferred_element_type=jnp.float32)
    grad_square = jnp.sum(jnp.square(grad_block.astype(jnp.float32)))
    dir_square = jnp.sum(jnp.square(direction))
    scaling = jnp.sqrt(grad_square + EPSILON) / jnp.sqrt(dir_square + EPSILON)
    update = (direction * scaling).astype(jnp.bfloat16)
    left_out, left_scale = requantize(left_new)
    right_out, right_scale = requantize(right_new)
    return (update, left_out, left_scale, right_out, right_scale)

def reference(gradient, left_codes, left_scales, right_codes, right_scales, left_root_codes, left_root_scales, right_root_codes, right_root_scales, owner_plan):
    update, left_out, left_scale, right_out, right_scale = lax.map(one_block, (gradient, left_codes, left_scales, right_codes, right_scales, left_root_codes, left_root_scales, right_root_codes, right_root_scales))
    inverse = jnp.zeros_like(owner_plan).at[owner_plan].set(jnp.arange(owner_plan.shape[0], dtype=jnp.int32))
    return (left_out[inverse], left_scale[inverse], right_out[inverse], right_scale[inverse], update)
```

```python
import functools

import jax
import jax.numpy as jnp
from jax import lax
from jax.experimental import pallas as pl
from jax.experimental.pallas import tpu as pltpu
from jax.sharding import PartitionSpec as P

DECAY = 0.95
EPSILON = 1e-06
RING = 4
HALVES = 2
MESH = pl.DeviceIdType.MESH
F32, BF16 = jnp.float32, jnp.bfloat16


def dot(a, b, dims):
    return lax.dot_general(a, b, (dims, ((), ())), preferred_element_type=F32)


def kernel(
    plan_ref, g_ref, lc_ref, ls_ref, rc_ref, rs_ref, lrc_ref, lrs_ref, rrc_ref, rrs_ref,
    nl_ref, nls_ref, nr_ref, nrs_ref, up_ref,
    ya, lroot, lifted, acc_l, acc_r, acc_f, dirs, cols, codes, scol, st, first, second, landed,
    info_v, info_s, sums_out, sums_in,
    ysend, yrecv, asend, arecv, psend, precv, isem,
):
    owners = first.shape[0]
    height, width = g_ref.shape[1:]
    half, part = height // 2, width // HALVES
    chunk = min(32, height)
    lanes = cols.shape[-1]
    piece_rows = first.shape[1]
    me, my_owner = lax.axis_index("mp"), lax.axis_index("dp")
    right, left = lax.rem(me + 1, RING), lax.rem(me + RING - 1, RING)

    barrier = pltpu.get_barrier_semaphore()
    for step in range(1, RING):
        pl.semaphore_signal(barrier, inc=1, device_id={"mp": lax.rem(me + step, RING)}, device_id_type=MESH)

    @pl.loop(1, owners)
    def _(step):
        pl.semaphore_signal(barrier, inc=1, device_id={"dp": lax.rem(my_owner + step, owners)}, device_id_type=MESH)

    blocks = plan_ref.shape[1]
    plan = jnp.transpose(jnp.broadcast_to(plan_ref[...], (blocks, blocks)))
    block = lax.broadcasted_iota(jnp.int32, (blocks, blocks), 0)
    owner = lax.broadcasted_iota(jnp.int32, (blocks, blocks), 1)
    target, anchor = lax.shift_right_logical(plan, 1), lax.shift_right_logical(block, 1)
    moving = target != anchor
    gives = moving & (anchor == owner)
    zero = jnp.zeros_like(block)
    info_v[0:1, :] = jnp.max(jnp.where(moving & (target == owner), anchor, zero), axis=0, keepdims=True)
    info_v[1:2, :] = jnp.max(jnp.where(gives, block & 1, zero), axis=0, keepdims=True)
    info_v[2:3, :] = jnp.max(jnp.where(gives, zero + 1, zero), axis=0, keepdims=True)
    to_scalars = pltpu.make_async_copy(info_v, info_s, isem)
    to_scalars.start()
    to_scalars.wait()
    vacancy, present = info_s[1, my_owner], info_s[2, my_owner] > 0
    slots = (vacancy, 1 - vacancy)

    def over_rows(body):
        @pl.loop(0, height // chunk)
        def _(r):
            body(pl.ds(pl.multiple_of(r * chunk, chunk), chunk))

    def wide(column):
        return jnp.concatenate([column] * (width // lanes), axis=1)

    for p in range(2):

        def stage(rows, p=p):
            ya[p, 0, rows, :] = g_ref[slots[p], rows, :]

        over_rows(stage)

    pl.semaphore_wait(barrier, owners - 1 + RING - 1)

    halves = (pl.ds(0, half), pl.ds(half, half))

    def hop(a, kind):
        source, target, which, to = (
            (0, 1, 0, right), (0, 1, 1, right), (0, 2, 0, left), (0, 2, 1, left), (1, 3, 0, right), (2, 3, 1, left),
        )[kind]
        return pltpu.make_async_remote_copy(
            src_ref=ya.at[a, source, halves[which]],
            dst_ref=ya.at[a, target, halves[which]],
            send_sem=ysend.at[a, kind],
            recv_sem=yrecv.at[a, kind],
            device_id={"mp": to},
            device_id_type=MESH,
        )

    def start(a, *kinds):
        for kind in kinds:
            hop(a, kind).start()

    def arrived(a, *kinds):
        for kind in kinds:
            hop(a, kind).wait_recv()

    start(0, 0, 3, 1, 2)

    for n, ref in enumerate((ls_ref, rs_ref, lrs_ref, rrs_ref)):
        both = ref[...].astype(F32)
        pair = (both[0:1, :], both[1:2, :])
        for p in range(2):
            row = jnp.where(vacancy == p, pair[0], pair[1])
            cols[n, p] = jnp.transpose(jnp.broadcast_to(row, (lanes, height)))
    for p in range(2):

        def roots(rows, p=p):
            lroot[p, rows, :] = (lrc_ref[slots[p], rows, :].astype(F32) * wide(cols[2, p, rows, :])).astype(BF16)
            ya[2 + p, 0, rows, :] = (rrc_ref[slots[p], rows, :].astype(F32) * wide(cols[3, p, rows, :])).astype(BF16)

        over_rows(roots)

    def squares(x):
        total = jnp.zeros((8, lanes), F32)
        x = jnp.sum(jnp.reshape(x * x, (x.shape[0] // 8, 8, width)), axis=0)
        for c in range(width // lanes):
            total = total + x[:, c * lanes : (c + 1) * lanes]
        return total

    for p in range(2):
        sums_out[p] = jnp.zeros((16, lanes), F32)

        def grad(rows, p=p):
            sums_out[p, 0:8, :] += squares(ya[p, 0, rows, :].astype(F32))

        over_rows(grad)

    deltas = (0, RING - 1, 1, 2)

    def columns(k):
        return pl.ds(pl.multiple_of(k * height, height), height)

    def band(p, rel):
        k = columns(lax.rem(me + deltas[rel], RING))
        acc_l[:, k] = dot(ya[p, 0], ya[p, rel], ((1,), (1,)))

        @pl.loop(0, RING)
        def _(n):
            cs = columns(n)
            x = ya[p, rel, :, cs]
            r = dot(ya[p, rel, :, columns(me)], x, ((0,), (0,)))
            f = dot(lroot[p, :, k], x, ((1,), (0,)))
            if rel == 0:
                acc_r[:, cs] = r
                acc_f[:, cs] = f
            else:
                acc_r[:, cs] += r
                acc_f[:, cs] += f

    def requantize(m, p, side, rows):
        scale = (jnp.max(jnp.abs(m), axis=1, keepdims=True) + EPSILON).astype(BF16).astype(F32)
        codes[p, side, rows, :] = (m / scale).astype(BF16)
        scol[p, side, rows, :] = jnp.broadcast_to(scale, (scale.shape[0], lanes))

    def statistics(p):
        def body(rows):
            lifted[p, rows, :] = acc_f[rows, :].astype(BF16)
            for side, (c, acc) in enumerate(((lc_ref, acc_l), (rc_ref, acc_r))):
                old = c[slots[p], rows, :].astype(F32) * wide(cols[side, p, rows, :])
                m = DECAY * old + acc[rows, :]
                if p == 0:
                    for h in range(HALVES):
                        st[h, side, rows, :] = m[:, h * part : (h + 1) * part].astype(BF16)
                requantize(m, p, side, rows)

        over_rows(body)

    pieces_down = height // piece_rows

    def piece(j):
        row = lax.div(j, HALVES)
        rows = pl.multiple_of(lax.rem(row, pieces_down) * piece_rows, piece_rows)
        return lax.rem(j, HALVES), lax.div(row, pieces_down), pl.ds(rows, piece_rows)

    mine = piece(my_owner)

    def spread(peer):
        return pltpu.make_async_remote_copy(
            src_ref=st.at[piece(peer)],
            dst_ref=first.at[my_owner],
            send_sem=asend.at[0],
            recv_sem=arecv.at[0],
            device_id={"dp": peer},
            device_id_type=MESH,
        )

    def deliver(peer):
        return pltpu.make_async_remote_copy(
            src_ref=second.at[peer],
            dst_ref=landed.at[mine],
            send_sem=asend.at[1],
            recv_sem=arecv.at[1],
            device_id={"dp": peer},
            device_id_type=MESH,
        )

    def all_but_mine(sem):
        others = first.at[pl.ds(0, owners - 1)]
        pltpu.make_async_copy(others, others, sem).wait()

    def spread_all():
        @pl.loop(1, owners)
        def _(step):
            spread(lax.rem(my_owner + step, owners)).start()

        first[my_owner] = st[mine]

    def deliver_all():
        all_but_mine(arecv.at[0])

        @pl.loop(0, owners)
        def _(d):
            second[d] = first[info_s[0, d]]

        @pl.loop(1, owners)
        def _(step):
            deliver(lax.rem(my_owner + step, owners)).start()

        landed[mine] = second[my_owner]

    def direction(p, rel):
        k = columns(lax.rem(me + deltas[rel], RING))

        @pl.loop(0, RING)
        def _(n):
            cs = columns(n)
            d = dot(lifted[p, :, k], ya[2 + p, rel, :, cs], ((1,), (0,)))
            if rel == 0:
                dirs[p, :, cs] = d
            else:
                dirs[p, :, cs] += d

    def share(p, step):
        return pltpu.make_async_remote_copy(
            src_ref=sums_out.at[p],
            dst_ref=sums_in.at[p, step - 1],
            send_sem=psend.at[p, step - 1],
            recv_sem=precv.at[p, step - 1],
            device_id={"mp": lax.rem(me + step, RING)},
            device_id_type=MESH,
        )

    def norms(p):
        def body(rows):
            sums_out[p, 8:16, :] += squares(dirs[p, rows, :])

        over_rows(body)
        for step in range(1, RING):
            share(p, step).start()

    arrived(0, 0, 3)
    start(0, 4, 5)
    band(0, 0)
    arrived(0, 1, 2)
    start(1, 0, 3, 1, 2)
    band(0, 1)
    band(0, 2)
    arrived(0, 4, 5)
    band(0, 3)
    statistics(0)
    spread_all()
    arrived(1, 0, 3)
    start(1, 4, 5)
    band(1, 0)
    arrived(1, 1, 2)
    start(2, 0, 3, 1, 2)
    band(1, 1)
    band(1, 2)
    arrived(1, 4, 5)
    band(1, 3)
    statistics(1)
    direction(0, 0)
    arrived(2, 0, 3)
    start(2, 4, 5)
    arrived(2, 1, 2)
    start(3, 0, 3, 1, 2)
    deliver_all()
    direction(0, 1)
    direction(0, 2)
    direction(1, 0)
    arrived(2, 4, 5)
    direction(0, 3)
    norms(0)
    arrived(3, 0, 3)
    start(3, 4, 5)
    arrived(3, 1, 2)
    direction(1, 1)
    direction(1, 2)
    arrived(3, 4, 5)
    direction(1, 3)
    norms(1)

    all_but_mine(arecv.at[1])

    def arriving(rows):
        for side, out in enumerate((nl_ref, nr_ref)):
            m = jnp.concatenate([landed[h, side, rows, :] for h in range(HALVES)], axis=1).astype(F32)
            scale = (jnp.max(jnp.abs(m), axis=1, keepdims=True) + EPSILON).astype(BF16).astype(F32)
            fresh = (m / scale).astype(BF16)
            first_code = jnp.where(present, fresh, codes[0, side, rows, :])
            other_code = codes[1, side, rows, :]
            out[0, rows, :] = jnp.where(vacancy == 0, first_code, other_code)
            out[1, rows, :] = jnp.where(vacancy == 0, other_code, first_code)
            scol[0, side, rows, :] = jnp.where(
                present, jnp.broadcast_to(scale, (scale.shape[0], lanes)), scol[0, side, rows, :]
            )

    over_rows(arriving)
    for side, out in enumerate((nls_ref, nrs_ref)):
        pair = [jnp.transpose(scol[p, side])[0:1, :] for p in range(2)]
        upper = jnp.where(vacancy == 0, pair[0], pair[1])
        lower = jnp.where(vacancy == 0, pair[1], pair[0])
        out[...] = jnp.concatenate([upper, lower], axis=0).astype(BF16)

    ratios = []
    for p in range(2):
        total = sums_out[p]
        for step in range(1, RING):
            share(p, step).wait_recv()
            total = total + sums_in[p, step - 1]
        grad_total = jnp.sum(total[0:8, :], keepdims=True)
        dir_total = jnp.sum(total[8:16, :], keepdims=True)
        ratios.append(jnp.sqrt(grad_total + EPSILON) / jnp.sqrt(dir_total + EPSILON))

    def grafted(rows):
        pair = [(dirs[p, rows, :] * ratios[p]).astype(BF16) for p in range(2)]
        up_ref[0, rows, :] = jnp.where(vacancy == 0, pair[0], pair[1])
        up_ref[1, rows, :] = jnp.where(vacancy == 0, pair[1], pair[0])

    over_rows(grafted)

    for a in range(4):
        for kind in range(6):
            hop(a, kind).wait_send()
    for p in range(2):
        for step in range(1, RING):
            share(p, step).wait_send()
    for phase in range(2):
        all_but_mine(asend.at[phase])


def local(*args):
    *arrays, plan = args
    slots, height, width = arrays[0].shape
    owners = lax.axis_size("dp")
    blocks = plan.shape[0]
    lanes = 128
    part = width // HALVES
    piece_rows = HALVES * 2 * height // owners
    big = jax.ShapeDtypeStruct((slots, height, width), BF16)
    small = jax.ShapeDtypeStruct((slots, height), BF16)
    vmem = pl.BlockSpec(memory_space=pltpu.VMEM)
    dma = pltpu.SemaphoreType.DMA
    return pl.pallas_call(
        kernel,
        out_shape=(big, small, big, small, big),
        in_specs=[vmem] * 10,
        out_specs=(vmem,) * 5,
        scratch_shapes=[
            pltpu.VMEM((4, RING, height, width), BF16),
            pltpu.VMEM((2, height, width), BF16),
            pltpu.VMEM((2, height, width), BF16),
            pltpu.VMEM((height, width), F32),
            pltpu.VMEM((height, width), F32),
            pltpu.VMEM((height, width), F32),
            pltpu.VMEM((2, height, width), F32),
            pltpu.VMEM((4, 2, height, lanes), F32),
            pltpu.VMEM((2, 2, height, width), BF16),
            pltpu.VMEM((2, 2, height, lanes), F32),
            pltpu.VMEM((HALVES, 2, height, part), BF16),
            pltpu.VMEM((owners, piece_rows, part), BF16),
            pltpu.VMEM((owners, piece_rows, part), BF16),
            pltpu.VMEM((HALVES, 2, height, part), BF16),
            pltpu.VMEM((8, blocks), jnp.int32),
            pltpu.SMEM((8, blocks), jnp.int32),
            pltpu.VMEM((2, 16, lanes), F32),
            pltpu.VMEM((2, RING - 1, 16, lanes), F32),
            dma((4, 6)),
            dma((4, 6)),
            dma((2,)),
            dma((2,)),
            dma((2, RING - 1)),
            dma((2, RING - 1)),
            dma,
        ],
        compiler_params=pltpu.CompilerParams(
            collective_id=0, has_side_effects=True, vmem_limit_bytes=52 * 1024 * 1024
        ),
        name="shampoo_step",
    )(plan.reshape(1, blocks), *arrays)


def solution(mesh):
    row_bands, rows = P("dp", "mp", None), P("dp", "mp")
    return jax.shard_map(
        local,
        mesh=mesh,
        in_specs=(row_bands, row_bands, rows, row_bands, rows, row_bands, rows, row_bands, rows, P()),
        out_specs=(row_bands, rows, row_bands, rows, row_bands),
        check_vma=False,
    )
```

```python
import jax
import jax.numpy as jnp
from jax import lax
from jax.experimental import pallas as pl
from jax.experimental.pallas import tpu as pltpu
from jax.sharding import PartitionSpec as P

DECAY = 0.95
EPSILON = 1e-06
RING = 4
MESH = pl.DeviceIdType.MESH
F32, BF16 = jnp.float32, jnp.bfloat16


def dot(a, b, dims):
    return lax.dot_general(a, b, (dims, ((), ())), preferred_element_type=F32)


def kernel(
    plan_hbm, g_hbm, lc_hbm, ls_hbm, rc_hbm, rs_hbm, lrc_hbm, lrs_hbm, rrc_hbm, rrs_hbm,
    nl_hbm, nls_hbm, nr_hbm, nrs_hbm, up_hbm,
    plan_ref, g_ref, lc_ref, ls_ref, rc_ref, rs_ref, lrc_ref, lrs_ref, rrc_ref, rrs_ref,
    nl_ref, nls_ref, nr_ref, nrs_ref, up_ref,
    ya, lroot, lifted, acc_l, acc_r, acc_f, dirs, cols, codes, scol, grafted, st, first, second, landed,
    info_v, info_s, sums_out, sums_in,
    ysend, yrecv, asend, arecv, psend, precv, isem, insem, outsem,
):
    owners = first.shape[0]
    height, width = g_ref.shape[1:]
    half = height // 2
    chunk = min(32, height)
    lanes = cols.shape[-1]
    groups = owners // (2 * RING)
    piece_rows = height // groups
    me, my_owner = lax.axis_index("mp"), lax.axis_index("dp")
    right, left = lax.rem(me + 1, RING), lax.rem(me + RING - 1, RING)

    def fetch(n, source, target):
        return pltpu.make_async_copy(source, target, insem.at[n])

    inputs = [
        fetch(n, *pair)
        for n, pair in enumerate(
            (
                (plan_hbm, plan_ref), (g_hbm, g_ref), (ls_hbm, ls_ref), (lc_hbm, lc_ref), (rs_hbm, rs_ref),
                (rc_hbm, rc_ref), (lrs_hbm, lrs_ref), (rrs_hbm, rrs_ref), (lrc_hbm, lrc_ref), (rrc_hbm, rrc_ref),
            )
        )
    ]
    for copy in inputs:
        copy.start()
    outputs = [
        pltpu.make_async_copy(source, target, outsem.at[n])
        for n, (source, target) in enumerate(
            ((nl_ref, nl_hbm), (nls_ref, nls_hbm), (nr_ref, nr_hbm), (nrs_ref, nrs_hbm), (up_ref, up_hbm))
        )
    ]

    barrier = pltpu.get_barrier_semaphore()
    for step in range(1, RING):
        pl.semaphore_signal(barrier, inc=1, device_id={"mp": lax.rem(me + step, RING)}, device_id_type=MESH)

    @pl.loop(1, owners)
    def _(step):
        pl.semaphore_signal(barrier, inc=1, device_id={"dp": lax.rem(my_owner + step, owners)}, device_id_type=MESH)

    inputs[0].wait()
    blocks = plan_ref.shape[1]
    plan = jnp.transpose(jnp.broadcast_to(plan_ref[...], (blocks, blocks)))
    block = lax.broadcasted_iota(jnp.int32, (blocks, blocks), 0)
    owner = lax.broadcasted_iota(jnp.int32, (blocks, blocks), 1)
    target, anchor = lax.shift_right_logical(plan, 1), lax.shift_right_logical(block, 1)
    moving = target != anchor
    gives = moving & (anchor == owner)
    zero = jnp.zeros_like(block)
    info_v[0:1, :] = jnp.max(jnp.where(moving & (target == owner), anchor, zero), axis=0, keepdims=True)
    info_v[1:2, :] = jnp.max(jnp.where(gives, block & 1, zero), axis=0, keepdims=True)
    info_v[2:3, :] = jnp.max(jnp.where(gives, zero + 1, zero), axis=0, keepdims=True)
    to_scalars = pltpu.make_async_copy(info_v, info_s, isem)
    to_scalars.start()
    to_scalars.wait()
    vacancy, present = info_s[1, my_owner], info_s[2, my_owner] > 0
    slots = (vacancy, 1 - vacancy)

    def over_rows(body):
        @pl.loop(0, height // chunk)
        def _(r):
            body(pl.ds(pl.multiple_of(r * chunk, chunk), chunk))

    def wide(column, columns=width):
        return jnp.concatenate([column] * (columns // lanes), axis=1) if columns > lanes else column[:, :columns]

    inputs[1].wait()
    for p in range(2):

        def stage(rows, p=p):
            ya[p, 0, rows, :] = g_ref[slots[p], rows, :]

        over_rows(stage)

    def scale_columns(n, ref):
        both = ref[...].astype(F32)
        pair = (both[0:1, :], both[1:2, :])
        for p in range(2):
            row = jnp.where(vacancy == p, pair[0], pair[1])
            cols[n, p] = jnp.transpose(jnp.broadcast_to(row, (lanes, height)))

    inputs[2].wait()
    scale_columns(0, ls_ref)
    inputs[3].wait()

    pl.semaphore_wait(barrier, owners - 1 + RING - 1)

    halves = (pl.ds(0, half), pl.ds(half, half))

    def hop(a, kind):
        source, target, which, to = (
            (0, 1, 0, right), (0, 1, 1, right), (0, 2, 0, left), (0, 2, 1, left), (1, 3, 0, right), (2, 3, 1, left),
        )[kind]
        return pltpu.make_async_remote_copy(
            src_ref=ya.at[a, source, halves[which]],
            dst_ref=ya.at[a, target, halves[which]],
            send_sem=ysend.at[a, kind],
            recv_sem=yrecv.at[a, kind],
            device_id={"mp": to},
            device_id_type=MESH,
        )

    def start(a, *kinds):
        for kind in kinds:
            hop(a, kind).start()

    def arrived(a, *kinds):
        for kind in kinds:
            hop(a, kind).wait_recv()

    start(0, 0, 3, 1, 2)

    deltas = (0, RING - 1, 1, 2)

    def columns(k):
        return pl.ds(pl.multiple_of(k * height, height), height)

    def piece(j):
        q = lax.div(j, 2)
        group = lax.rem(q, groups)
        tile = lax.rem(lax.div(q, groups) + group, RING)
        return lax.rem(j, 2), tile, pl.ds(pl.multiple_of(group * piece_rows, piece_rows), piece_rows)

    mine = piece(my_owner)

    def spread(side, tile):
        @pl.loop(0, groups)
        def _(step):
            group = lax.rem(lax.rem(lax.div(my_owner, 2), groups) + step, groups)
            peer = (lax.rem(tile + RING * groups - group, RING) * groups + group) * 2 + side
            source = st.at[side, tile, pl.ds(pl.multiple_of(group * piece_rows, piece_rows), piece_rows)]

            @pl.when(peer != my_owner)
            def _():
                pltpu.make_async_remote_copy(
                    src_ref=source,
                    dst_ref=first.at[my_owner],
                    send_sem=asend.at[0],
                    recv_sem=arecv.at[0],
                    device_id={"dp": peer},
                    device_id_type=MESH,
                ).start()

    def all_but_mine(sem):
        others = first.at[pl.ds(0, owners - 1)]
        pltpu.make_async_copy(others, others, sem).wait()

    def deliver_all():
        first[my_owner] = st[mine]
        all_but_mine(arecv.at[0])

        @pl.loop(0, owners)
        def _(d):
            second[d] = first[info_s[0, d]]

        @pl.loop(1, owners)
        def _(step):
            peer = lax.rem(my_owner + step, owners)
            pltpu.make_async_remote_copy(
                src_ref=second.at[peer],
                dst_ref=landed.at[mine],
                send_sem=asend.at[1],
                recv_sem=arecv.at[1],
                device_id={"dp": peer},
                device_id_type=MESH,
            ).start()

        landed[mine] = second[my_owner]

    def left_tile(p, rel):
        k = columns(lax.rem(me + deltas[rel], RING))
        tile = dot(ya[p, 0], ya[p, rel], ((1,), (1,)))
        old = lc_ref[slots[p], :, k].astype(F32) * wide(cols[0, p], height)
        m = DECAY * old + tile
        acc_l[p, :, k] = m
        if p == 0:
            st[0, rel] = m.astype(BF16)
            spread(0, rel)

    def band(p, rel):
        k = columns(lax.rem(me + deltas[rel], RING))
        both = jnp.concatenate([jnp.transpose(ya[p, rel, :, columns(me)]), lroot[p, :, k]], axis=0)

        @pl.loop(0, RING)
        def _(n):
            cs = columns(n)
            y = dot(both, ya[p, rel, :, cs], ((1,), (0,)))
            if rel == 0:
                acc_r[p, :, cs] = y[:height]
                acc_f[:, cs] = y[height:]
            else:
                acc_r[p, :, cs] += y[:height]
                acc_f[:, cs] += y[height:]

    def right_tiles(p):
        @pl.loop(0, RING)
        def _(n):
            cs = columns(n)
            m = DECAY * (rc_ref[slots[p], :, cs].astype(F32) * wide(cols[1, p], height)) + acc_r[p, :, cs]
            acc_r[p, :, cs] = m
            if p == 0:
                st[1, n] = m.astype(BF16)
                spread(1, n)

    def requantize(m):
        scale = (jnp.max(jnp.abs(m), axis=1, keepdims=True) + EPSILON).astype(BF16).astype(F32)
        return (m / scale).astype(BF16), jnp.broadcast_to(scale, (scale.shape[0], lanes))

    def finish(p):
        def body(rows):
            lifted[p, rows, :] = acc_f[rows, :].astype(BF16)
            for side, acc in enumerate((acc_l, acc_r)):
                codes[p, side, rows, :], scol[p, side, rows, :] = requantize(acc[p, rows, :])

        over_rows(body)

    def roots(p):
        def body(rows):
            lroot[p, rows, :] = (lrc_ref[slots[p], rows, :].astype(F32) * wide(cols[2, p, rows, :])).astype(BF16)
            ya[2 + p, 0, rows, :] = (rrc_ref[slots[p], rows, :].astype(F32) * wide(cols[3, p, rows, :])).astype(BF16)

        over_rows(body)

    def squares(x):
        total = jnp.zeros((8, lanes), F32)
        x = jnp.sum(jnp.reshape(x * x, (x.shape[0] // 8, 8, width)), axis=0)
        for c in range(width // lanes):
            total = total + x[:, c * lanes : (c + 1) * lanes]
        return total

    def gradient_norm(p):
        sums_out[p] = jnp.zeros((16, lanes), F32)

        def body(rows):
            sums_out[p, 0:8, :] += squares(ya[p, 0, rows, :].astype(F32))

        over_rows(body)

    def direction(p, rel):
        k = columns(lax.rem(me + deltas[rel], RING))

        @pl.loop(0, RING)
        def _(n):
            cs = columns(n)
            d = dot(lifted[p, :, k], ya[2 + p, rel, :, cs], ((1,), (0,)))
            if rel == 0:
                dirs[p, :, cs] = d
            else:
                dirs[p, :, cs] += d

    def share(p, step):
        return pltpu.make_async_remote_copy(
            src_ref=sums_out.at[p],
            dst_ref=sums_in.at[p, step - 1],
            send_sem=psend.at[p, step - 1],
            recv_sem=precv.at[p, step - 1],
            device_id={"mp": lax.rem(me + step, RING)},
            device_id_type=MESH,
        )

    def norms(p):
        def body(rows):
            sums_out[p, 8:16, :] += squares(dirs[p, rows, :])

        over_rows(body)
        for step in range(1, RING):
            share(p, step).start()

    def ratio(p):
        total = sums_out[p]
        for step in range(1, RING):
            share(p, step).wait_recv()
            total = total + sums_in[p, step - 1]
        grad_total = jnp.sum(total[0:8, :], keepdims=True)
        dir_total = jnp.sum(total[8:16, :], keepdims=True)
        return jnp.sqrt(grad_total + EPSILON) / jnp.sqrt(dir_total + EPSILON)

    def graft(p):
        r = ratio(p)

        def body(rows):
            update = (dirs[p, rows, :] * r).astype(BF16)
            if p == 0:
                grafted[rows, :] = update
            else:
                up_ref[0, rows, :] = jnp.where(vacancy == 0, grafted[rows, :], update)
                up_ref[1, rows, :] = jnp.where(vacancy == 0, update, grafted[rows, :])

        over_rows(body)

    left_tile(0, 0)
    for n in range(4, 10):
        inputs[n].wait()
    scale_columns(1, rs_ref)
    scale_columns(2, lrs_ref)
    scale_columns(3, rrs_ref)
    roots(0)
    arrived(0, 0, 3)
    start(0, 4, 5)
    band(0, 0)
    roots(1)
    gradient_norm(0)
    arrived(0, 1, 2)
    start(1, 0, 3, 1, 2)
    left_tile(0, 1)
    left_tile(0, 2)
    band(0, 1)
    band(0, 2)
    arrived(0, 4, 5)
    left_tile(0, 3)
    band(0, 3)
    right_tiles(0)
    finish(0)
    gradient_norm(1)
    left_tile(1, 0)
    band(1, 0)
    arrived(1, 0, 3)
    start(1, 4, 5)
    start(2, 0, 3, 1, 2)
    direction(0, 0)
    deliver_all()
    arrived(1, 1, 2)
    for rel in (1, 2):
        left_tile(1, rel)
        band(1, rel)
    arrived(1, 4, 5)
    left_tile(1, 3)
    band(1, 3)
    right_tiles(1)
    finish(1)
    arrived(2, 0, 3)
    start(2, 4, 5)
    start(3, 0, 3, 1, 2)
    direction(1, 0)
    arrived(2, 1, 2)
    direction(0, 1)
    direction(0, 2)
    arrived(2, 4, 5)
    direction(0, 3)
    norms(0)
    arrived(3, 0, 3)
    start(3, 4, 5)
    graft(0)

    all_but_mine(arecv.at[1])

    def arriving(rows):
        for side, out in enumerate((nl_ref, nr_ref)):
            m = [landed[side, t, rows, :].astype(F32) for t in range(RING)]
            top = jnp.maximum(jnp.maximum(jnp.abs(m[0]), jnp.abs(m[1])), jnp.maximum(jnp.abs(m[2]), jnp.abs(m[3])))
            scale = (jnp.max(top, axis=1, keepdims=True) + EPSILON).astype(BF16).astype(F32)
            for t in range(RING):
                cs = columns(lax.rem(me + deltas[t], RING)) if side == 0 else pl.ds(t * height, height)
                fresh = (m[t] / scale).astype(BF16)
                first_code = jnp.where(present, fresh, codes[0, side, rows, cs])
                other_code = codes[1, side, rows, cs]
                out[0, rows, cs] = jnp.where(vacancy == 0, first_code, other_code)
                out[1, rows, cs] = jnp.where(vacancy == 0, other_code, first_code)
            scol[0, side, rows, :] = jnp.where(
                present, jnp.broadcast_to(scale, (scale.shape[0], lanes)), scol[0, side, rows, :]
            )

    over_rows(arriving)
    for side, out in enumerate((nls_ref, nrs_ref)):
        pair = [jnp.transpose(scol[p, side])[0:1, :] for p in range(2)]
        upper = jnp.where(vacancy == 0, pair[0], pair[1])
        lower = jnp.where(vacancy == 0, pair[1], pair[0])
        out[...] = jnp.concatenate([upper, lower], axis=0).astype(BF16)
    for copy in outputs[:4]:
        copy.start()

    arrived(3, 1, 2)
    direction(1, 1)
    direction(1, 2)
    for a in range(3):
        for kind in range(6):
            hop(a, kind).wait_send()
    for phase in range(2):
        all_but_mine(asend.at[phase])
    arrived(3, 4, 5)
    direction(1, 3)
    norms(1)
    graft(1)
    outputs[4].start()

    for kind in range(6):
        hop(3, kind).wait_send()
    for p in range(2):
        for step in range(1, RING):
            share(p, step).wait_send()
    for copy in outputs:
        copy.wait()


def results_to_hbm(*refs):
    n = len(refs[:-2]) // 3
    insem, outsem = refs[-2:]
    parts = []
    for i in range(n):
        source, target, held = refs[i], refs[n + i], refs[2 * n + i]
        slices = [pl.ds(0, 1), pl.ds(1, 1)] if len(held.shape) == 3 else [pl.ds(0, held.shape[0])]
        for part in slices:
            m = len(parts)
            parts.append(
                (
                    pltpu.make_async_copy(source.at[part], held.at[part], insem.at[m]),
                    pltpu.make_async_copy(held.at[part], target.at[part], outsem.at[m]),
                )
            )
    for inward, _ in parts:
        inward.start()
    for inward, outward in parts:
        inward.wait()
        outward.start()
    for _, outward in parts:
        outward.wait()


def local(*args):
    *arrays, plan = args
    slots, height, width = arrays[0].shape
    owners = lax.axis_size("dp")
    blocks = plan.shape[0]
    lanes = 128
    piece_rows = height // (owners // (2 * RING))
    big = jax.ShapeDtypeStruct((slots, height, width), BF16)
    small = jax.ShapeDtypeStruct((slots, height), BF16)
    outs = (big, small, big, small, big)
    hbm = pl.BlockSpec(memory_space=pl.ANY)
    dma = pltpu.SemaphoreType.DMA
    held = [plan.reshape(1, blocks), *arrays]
    results = pl.pallas_call(
        kernel,
        out_shape=outs,
        in_specs=[hbm] * 10,
        out_specs=(hbm,) * 5,
        scratch_shapes=[
            *(pltpu.VMEM(x.shape, x.dtype) for x in (*held, *outs)),
            pltpu.VMEM((4, RING, height, width), BF16),
            pltpu.VMEM((2, height, width), BF16),
            pltpu.VMEM((2, height, width), BF16),
            pltpu.VMEM((2, height, width), F32),
            pltpu.VMEM((2, height, width), F32),
            pltpu.VMEM((height, width), F32),
            pltpu.VMEM((2, height, width), F32),
            pltpu.VMEM((4, 2, height, lanes), F32),
            pltpu.VMEM((2, 2, height, width), BF16),
            pltpu.VMEM((2, 2, height, lanes), F32),
            pltpu.VMEM((height, width), BF16),
            pltpu.VMEM((2, RING, height, height), BF16),
            pltpu.VMEM((owners, piece_rows, height), BF16),
            pltpu.VMEM((owners, piece_rows, height), BF16),
            pltpu.VMEM((2, RING, height, height), BF16),
            pltpu.VMEM((8, blocks), jnp.int32),
            pltpu.SMEM((8, blocks), jnp.int32),
            pltpu.VMEM((2, 16, lanes), F32),
            pltpu.VMEM((2, RING - 1, 16, lanes), F32),
            dma((4, 6)),
            dma((4, 6)),
            dma((2,)),
            dma((2,)),
            dma((2, RING - 1)),
            dma((2, RING - 1)),
            dma,
            dma((10,)),
            dma((5,)),
        ],
        compiler_params=pltpu.CompilerParams(
            collective_id=0, has_side_effects=True, vmem_limit_bytes=60 * 1024 * 1024
        ),
        name="shampoo_step",
    )(*held)
    return pl.pallas_call(
        results_to_hbm,
        out_shape=outs,
        in_specs=[hbm] * 5,
        out_specs=(hbm,) * 5,
        scratch_shapes=[*(pltpu.VMEM(x.shape, x.dtype) for x in outs), dma((8,)), dma((8,))],
        compiler_params=pltpu.CompilerParams(vmem_limit_bytes=60 * 1024 * 1024),
        name="results_to_hbm",
    )(*results)


def solution(mesh):
    row_bands, rows = P("dp", "mp", None), P("dp", "mp")
    return jax.shard_map(
        local,
        mesh=mesh,
        in_specs=(row_bands, row_bands, rows, row_bands, rows, row_bands, rows, row_bands, rows, P()),
        out_specs=(row_bands, rows, row_bands, rows, row_bands),
        check_vma=False,
    )
```

```python
import jax
import jax.numpy as jnp
from jax import lax
from jax.experimental import pallas as pl
from jax.experimental.pallas import tpu as pltpu
from jax.sharding import PartitionSpec as P

DECAY = 0.95
EPSILON = 1e-06
RING = 4
MESH = pl.DeviceIdType.MESH
F32, BF16 = jnp.float32, jnp.bfloat16


def dot(a, b, dims):
    return lax.dot_general(a, b, (dims, ((), ())), preferred_element_type=F32)


def kernel(
    plan_hbm, g_hbm, lc_hbm, ls_hbm, rc_hbm, rs_hbm, lrc_hbm, lrs_hbm, rrc_hbm, rrs_hbm,
    nl_hbm, nls_hbm, nr_hbm, nrs_hbm, up_hbm,
    plan_ref, g_ref, lc_ref, ls_ref, rc_ref, rs_ref, lrc_ref, lrs_ref, rrc_ref, rrs_ref,
    nl_ref, nls_ref, nr_ref, nrs_ref, up_ref,
    ya, lroot, lifted, acc_l, acc_r, acc_f, dirs, cols, codes, scol, grafted, st, first, second, landed,
    plan_s, info_v, info_s, sums_out, sums_in,
    ysend, yrecv, asend, arecv, psend, precv, isem, insem, outsem, word,
):
    owners = first.shape[0]
    height, width = g_ref.shape[1:]
    half = height // 2
    chunk = min(32, height)
    lanes = cols.shape[-1]
    groups = owners // (2 * RING)
    piece_rows = height // groups
    me, my_owner = lax.axis_index("mp"), lax.axis_index("dp")
    right, left = lax.rem(me + 1, RING), lax.rem(me + RING - 1, RING)

    def fetch(n, source, target):
        return pltpu.make_async_copy(source, target, insem.at[n])

    inputs = [
        fetch(n, *pair)
        for n, pair in enumerate(
            (
                (plan_hbm, plan_s), (g_hbm, g_ref), (ls_hbm, ls_ref), (lc_hbm, lc_ref), (rs_hbm, rs_ref),
                (rc_hbm, rc_ref), (lrs_hbm, lrs_ref), (rrs_hbm, rrs_ref), (lrc_hbm, lrc_ref), (rrc_hbm, rrc_ref),
                (plan_hbm, plan_ref),
            )
        )
    ]
    for copy in inputs:
        copy.start()
    outputs = [
        pltpu.make_async_copy(source, target, outsem.at[n])
        for n, (source, target) in enumerate(
            ((nl_ref, nl_hbm), (nls_ref, nls_hbm), (nr_ref, nr_hbm), (nrs_ref, nrs_hbm), (up_ref, up_hbm))
        )
    ]

    core, z = lax.rem(my_owner, 2), lax.rem(lax.div(my_owner, 2), groups)
    x = lax.div(my_owner, 2 * groups)

    def owner_at(x, z, core):
        return {"dp": (x * groups + z) * 2 + core}

    beside_z = [owner_at(x, lax.rem(z + step, groups), core) for step in (1, groups - 1)] if groups > 1 else []
    beside_x = [owner_at(lax.rem(x + step, RING), z, core) for step in range(1, RING)]
    other_core = [owner_at(x, z, 1 - core)]
    ring = [{"mp": lax.rem(me + step, RING)} for step in range(1, RING)]
    near = [*ring, *beside_x, *beside_z, *other_core]
    barrier = pltpu.get_barrier_semaphore()
    for device in near:
        pl.semaphore_signal(barrier, inc=1, device_id=device, device_id_type=MESH)
    rounds = [beside_z] * 3 + [other_core, beside_x]

    def tell(n):
        for device in rounds[n]:
            pl.semaphore_signal(word.at[n], inc=1, device_id=device, device_id_type=MESH)

    def hear(n):
        if rounds[n]:
            pl.semaphore_wait(word.at[n], len(rounds[n]))

    inputs[0].wait()
    moves = [lax.shift_right_logical(plan_s[0, 2 * my_owner + slot], 1) != my_owner for slot in range(2)]
    vacancy, present = jnp.where(moves[1], 1, 0), moves[0] | moves[1]
    slots = (vacancy, 1 - vacancy)

    def routing():
        inputs[10].wait()
        blocks = plan_ref.shape[1]
        plan = jnp.transpose(jnp.broadcast_to(plan_ref[...], (blocks, blocks)))
        block = lax.broadcasted_iota(jnp.int32, (blocks, blocks), 0)
        owner = lax.broadcasted_iota(jnp.int32, (blocks, blocks), 1)
        target, anchor = lax.shift_right_logical(plan, 1), lax.shift_right_logical(block, 1)
        arrives = (target != anchor) & (target == owner)
        info_v[0:1, :] = jnp.max(jnp.where(arrives, anchor, jnp.zeros_like(block)), axis=0, keepdims=True)
        pltpu.make_async_copy(info_v, info_s, isem).start()

    def over_rows(body):
        @pl.loop(0, height // chunk)
        def _(r):
            body(pl.ds(pl.multiple_of(r * chunk, chunk), chunk))

    def wide(column, columns=width):
        return jnp.concatenate([column] * (columns // lanes), axis=1) if columns > lanes else column[:, :columns]

    def stage(p):
        def body(rows):
            ya[p, 0, rows, :] = g_ref[slots[p], rows, :]

        over_rows(body)

    def scale_columns(n, ref):
        both = ref[...].astype(F32)
        pair = (both[0:1, :], both[1:2, :])
        for p in range(2):
            row = jnp.where(vacancy == p, pair[0], pair[1])
            cols[n, p] = jnp.transpose(jnp.broadcast_to(row, (lanes, height)))

    inputs[1].wait()
    stage(0)
    pl.semaphore_wait(barrier, len(near))

    halves = (pl.ds(0, half), pl.ds(half, half))

    def hop(a, kind):
        source, target, which, to = (
            (0, 1, 0, right), (0, 1, 1, right), (0, 2, 0, left), (0, 2, 1, left), (1, 3, 0, right), (2, 3, 1, left),
        )[kind]
        return pltpu.make_async_remote_copy(
            src_ref=ya.at[a, source, halves[which]],
            dst_ref=ya.at[a, target, halves[which]],
            send_sem=ysend.at[a, kind],
            recv_sem=yrecv.at[a, kind],
            device_id={"mp": to},
            device_id_type=MESH,
        )

    def start(a, *kinds):
        for kind in kinds:
            hop(a, kind).start()

    def arrived(a, *kinds):
        for kind in kinds:
            hop(a, kind).wait_recv()

    start(0, 0, 3, 1, 2)

    deltas = (0, RING - 1, 1, 2)

    def columns(k):
        return pl.ds(pl.multiple_of(k * height, height), height)

    def piece(j):
        q = lax.div(j, 2)
        group = lax.rem(q, groups)
        tile = lax.rem(lax.div(q, groups) + group, RING)
        return lax.rem(j, 2), tile, pl.ds(pl.multiple_of(group * piece_rows, piece_rows), piece_rows)

    mine = piece(my_owner)

    def spread(side, tile):
        @pl.loop(0, groups)
        def _(step):
            group = lax.rem(lax.rem(lax.div(my_owner, 2), groups) + step, groups)
            peer = (lax.rem(tile + RING * groups - group, RING) * groups + group) * 2 + side
            source = st.at[side, tile, pl.ds(pl.multiple_of(group * piece_rows, piece_rows), piece_rows)]

            @pl.when(peer != my_owner)
            def _():
                pltpu.make_async_remote_copy(
                    src_ref=source,
                    dst_ref=first.at[my_owner],
                    send_sem=asend.at[0],
                    recv_sem=arecv.at[0],
                    device_id={"dp": peer},
                    device_id_type=MESH,
                ).start()

    def all_but_mine(sem):
        others = first.at[pl.ds(0, owners - 1)]
        pltpu.make_async_copy(others, others, sem).wait()

    def deliver_all():
        pltpu.make_async_copy(info_v, info_s, isem).wait()
        first[my_owner] = st[mine]
        all_but_mine(arecv.at[0])

        @pl.loop(0, owners)
        def _(d):
            second[d] = first[info_s[0, d]]

        @pl.loop(1, owners)
        def _(step):
            peer = lax.rem(my_owner + step, owners)
            pltpu.make_async_remote_copy(
                src_ref=second.at[peer],
                dst_ref=landed.at[mine],
                send_sem=asend.at[1],
                recv_sem=arecv.at[1],
                device_id={"dp": peer},
                device_id_type=MESH,
            ).start()

        landed[mine] = second[my_owner]

    def left_tile(p, rel):
        k = columns(lax.rem(me + deltas[rel], RING))
        tile = dot(ya[p, 0], ya[p, rel], ((1,), (1,)))
        old = lc_ref[slots[p], :, k].astype(F32) * wide(cols[0, p], height)
        m = DECAY * old + tile
        acc_l[p, :, k] = m
        if p == 0:
            st[0, rel] = m.astype(BF16)
            spread(0, rel)

    def band(p, rel):
        k = columns(lax.rem(me + deltas[rel], RING))
        both = jnp.concatenate([jnp.transpose(ya[p, rel, :, columns(me)]), lroot[p, :, k]], axis=0)

        @pl.loop(0, RING)
        def _(n):
            cs = columns(n)
            y = dot(both, ya[p, rel, :, cs], ((1,), (0,)))
            if rel == 0:
                acc_r[p, :, cs] = y[:height]
                acc_f[:, cs] = y[height:]
            else:
                acc_r[p, :, cs] += y[:height]
                acc_f[:, cs] += y[height:]

    def right_tiles(p):
        @pl.loop(0, RING)
        def _(n):
            cs = columns(n)
            m = DECAY * (rc_ref[slots[p], :, cs].astype(F32) * wide(cols[1, p], height)) + acc_r[p, :, cs]
            acc_r[p, :, cs] = m
            if p == 0:
                st[1, n] = m.astype(BF16)
                spread(1, n)

    def requantize(m):
        scale = (jnp.max(jnp.abs(m), axis=1, keepdims=True) + EPSILON).astype(BF16).astype(F32)
        return (m / scale).astype(BF16), jnp.broadcast_to(scale, (scale.shape[0], lanes))

    def finish(p):
        def body(rows):
            lifted[p, rows, :] = acc_f[rows, :].astype(BF16)
            for side, acc in enumerate((acc_l, acc_r)):
                codes[p, side, rows, :], scol[p, side, rows, :] = requantize(acc[p, rows, :])

        over_rows(body)

    def roots(p):
        def body(rows):
            lroot[p, rows, :] = (lrc_ref[slots[p], rows, :].astype(F32) * wide(cols[2, p, rows, :])).astype(BF16)
            ya[2 + p, 0, rows, :] = (rrc_ref[slots[p], rows, :].astype(F32) * wide(cols[3, p, rows, :])).astype(BF16)

        over_rows(body)

    def squares(x):
        total = jnp.zeros((8, lanes), F32)
        x = jnp.sum(jnp.reshape(x * x, (x.shape[0] // 8, 8, width)), axis=0)
        for c in range(width // lanes):
            total = total + x[:, c * lanes : (c + 1) * lanes]
        return total

    def gradient_norm(p):
        sums_out[p] = jnp.zeros((16, lanes), F32)

        def body(rows):
            sums_out[p, 0:8, :] += squares(ya[p, 0, rows, :].astype(F32))

        over_rows(body)

    def direction(p, rel):
        k = columns(lax.rem(me + deltas[rel], RING))

        @pl.loop(0, RING)
        def _(n):
            cs = columns(n)
            d = dot(lifted[p, :, k], ya[2 + p, rel, :, cs], ((1,), (0,)))
            if rel == 0:
                dirs[p, :, cs] = d
            else:
                dirs[p, :, cs] += d

    def share(p, step):
        return pltpu.make_async_remote_copy(
            src_ref=sums_out.at[p],
            dst_ref=sums_in.at[p, step - 1],
            send_sem=psend.at[p, step - 1],
            recv_sem=precv.at[p, step - 1],
            device_id={"mp": lax.rem(me + step, RING)},
            device_id_type=MESH,
        )

    def norms(p):
        def body(rows):
            sums_out[p, 8:16, :] += squares(dirs[p, rows, :])

        over_rows(body)
        for step in range(1, RING):
            share(p, step).start()

    def ratio(p):
        total = sums_out[p]
        for step in range(1, RING):
            share(p, step).wait_recv()
            total = total + sums_in[p, step - 1]
        grad_total = jnp.sum(total[0:8, :], keepdims=True)
        dir_total = jnp.sum(total[8:16, :], keepdims=True)
        return jnp.sqrt(grad_total + EPSILON) / jnp.sqrt(dir_total + EPSILON)

    def graft(p):
        r = ratio(p)

        def body(rows):
            update = (dirs[p, rows, :] * r).astype(BF16)
            if p == 0:
                grafted[rows, :] = update
            else:
                up_ref[0, rows, :] = jnp.where(vacancy == 0, grafted[rows, :], update)
                up_ref[1, rows, :] = jnp.where(vacancy == 0, update, grafted[rows, :])

        over_rows(body)

    tell(0)
    stage(1)
    for n in range(2, 10):
        inputs[n].wait()
    scale_columns(0, ls_ref)
    scale_columns(1, rs_ref)
    scale_columns(2, lrs_ref)
    hear(0)
    tell(1)
    scale_columns(3, rrs_ref)
    routing()
    hear(1)
    tell(2)
    roots(0)
    hear(2)
    tell(3)
    gradient_norm(0)
    hear(3)
    tell(4)
    arrived(0, 0, 3)
    start(0, 4, 5)
    hear(4)
    left_tile(0, 0)
    band(0, 0)
    roots(1)
    arrived(0, 1, 2)
    start(1, 0, 3, 1, 2)
    left_tile(0, 1)
    left_tile(0, 2)
    band(0, 1)
    band(0, 2)
    arrived(0, 4, 5)
    left_tile(0, 3)
    band(0, 3)
    right_tiles(0)
    finish(0)
    gradient_norm(1)
    left_tile(1, 0)
    band(1, 0)
    arrived(1, 0, 3)
    start(1, 4, 5)
    start(2, 0, 3, 1, 2)
    direction(0, 0)
    deliver_all()
    arrived(1, 1, 2)
    for rel in (1, 2):
        left_tile(1, rel)
        band(1, rel)
    arrived(1, 4, 5)
    left_tile(1, 3)
    band(1, 3)
    right_tiles(1)
    finish(1)
    arrived(2, 0, 3)
    start(2, 4, 5)
    start(3, 0, 3, 1, 2)
    direction(1, 0)
    arrived(2, 1, 2)
    direction(0, 1)
    direction(0, 2)
    arrived(2, 4, 5)
    direction(0, 3)
    norms(0)
    arrived(3, 0, 3)
    start(3, 4, 5)
    graft(0)

    all_but_mine(arecv.at[1])

    def arriving(rows):
        for side, out in enumerate((nl_ref, nr_ref)):
            m = [landed[side, t, rows, :].astype(F32) for t in range(RING)]
            top = jnp.maximum(jnp.maximum(jnp.abs(m[0]), jnp.abs(m[1])), jnp.maximum(jnp.abs(m[2]), jnp.abs(m[3])))
            scale = (jnp.max(top, axis=1, keepdims=True) + EPSILON).astype(BF16).astype(F32)
            for t in range(RING):
                cs = columns(lax.rem(me + deltas[t], RING)) if side == 0 else pl.ds(t * height, height)
                fresh = (m[t] / scale).astype(BF16)
                first_code = jnp.where(present, fresh, codes[0, side, rows, cs])
                other_code = codes[1, side, rows, cs]
                out[0, rows, cs] = jnp.where(vacancy == 0, first_code, other_code)
                out[1, rows, cs] = jnp.where(vacancy == 0, other_code, first_code)
            scol[0, side, rows, :] = jnp.where(
                present, jnp.broadcast_to(scale, (scale.shape[0], lanes)), scol[0, side, rows, :]
            )

    over_rows(arriving)
    for side, out in enumerate((nls_ref, nrs_ref)):
        pair = [jnp.transpose(scol[p, side])[0:1, :] for p in range(2)]
        upper = jnp.where(vacancy == 0, pair[0], pair[1])
        lower = jnp.where(vacancy == 0, pair[1], pair[0])
        out[...] = jnp.concatenate([upper, lower], axis=0).astype(BF16)
    for copy in outputs[:4]:
        copy.start()

    arrived(3, 1, 2)
    direction(1, 1)
    direction(1, 2)
    for a in range(3):
        for kind in range(6):
            hop(a, kind).wait_send()
    for phase in range(2):
        all_but_mine(asend.at[phase])
    arrived(3, 4, 5)
    direction(1, 3)
    norms(1)
    graft(1)
    outputs[4].start()

    for kind in range(6):
        hop(3, kind).wait_send()
    for p in range(2):
        for step in range(1, RING):
            share(p, step).wait_send()
    for copy in outputs:
        copy.wait()


def results_to_hbm(*refs):
    n = len(refs[:-2]) // 3
    insem, outsem = refs[-2:]
    parts = []
    for i in range(n):
        source, target, held = refs[i], refs[n + i], refs[2 * n + i]
        slices = [pl.ds(0, 1), pl.ds(1, 1)] if len(held.shape) == 3 else [pl.ds(0, held.shape[0])]
        for part in slices:
            m = len(parts)
            parts.append(
                (
                    pltpu.make_async_copy(source.at[part], held.at[part], insem.at[m]),
                    pltpu.make_async_copy(held.at[part], target.at[part], outsem.at[m]),
                )
            )
    for inward, _ in parts:
        inward.start()
    for inward, outward in parts:
        inward.wait()
        outward.start()
    for _, outward in parts:
        outward.wait()


def local(*args):
    *arrays, plan = args
    slots, height, width = arrays[0].shape
    owners = lax.axis_size("dp")
    blocks = plan.shape[0]
    lanes = 128
    piece_rows = height // (owners // (2 * RING))
    big = jax.ShapeDtypeStruct((slots, height, width), BF16)
    small = jax.ShapeDtypeStruct((slots, height), BF16)
    outs = (big, small, big, small, big)
    hbm = pl.BlockSpec(memory_space=pl.ANY)
    dma = pltpu.SemaphoreType.DMA
    held = [plan.reshape(1, blocks), *arrays]
    results = pl.pallas_call(
        kernel,
        out_shape=outs,
        in_specs=[hbm] * 10,
        out_specs=(hbm,) * 5,
        scratch_shapes=[
            *(pltpu.VMEM(x.shape, x.dtype) for x in (*held, *outs)),
            pltpu.VMEM((4, RING, height, width), BF16),
            pltpu.VMEM((2, height, width), BF16),
            pltpu.VMEM((2, height, width), BF16),
            pltpu.VMEM((2, height, width), F32),
            pltpu.VMEM((2, height, width), F32),
            pltpu.VMEM((height, width), F32),
            pltpu.VMEM((2, height, width), F32),
            pltpu.VMEM((4, 2, height, lanes), F32),
            pltpu.VMEM((2, 2, height, width), BF16),
            pltpu.VMEM((2, 2, height, lanes), F32),
            pltpu.VMEM((height, width), BF16),
            pltpu.VMEM((2, RING, height, height), BF16),
            pltpu.VMEM((owners, piece_rows, height), BF16),
            pltpu.VMEM((owners, piece_rows, height), BF16),
            pltpu.VMEM((2, RING, height, height), BF16),
            pltpu.SMEM((1, blocks), jnp.int32),
            pltpu.VMEM((8, blocks), jnp.int32),
            pltpu.SMEM((8, blocks), jnp.int32),
            pltpu.VMEM((2, 16, lanes), F32),
            pltpu.VMEM((2, RING - 1, 16, lanes), F32),
            dma((4, 6)),
            dma((4, 6)),
            dma((2,)),
            dma((2,)),
            dma((2, RING - 1)),
            dma((2, RING - 1)),
            dma,
            dma((11,)),
            dma((5,)),
            pltpu.SemaphoreType.REGULAR((5,)),
        ],
        compiler_params=pltpu.CompilerParams(
            collective_id=0, has_side_effects=True, vmem_limit_bytes=60 * 1024 * 1024
        ),
        name="shampoo_step",
    )(*held)
    return pl.pallas_call(
        results_to_hbm,
        out_shape=outs,
        in_specs=[hbm] * 5,
        out_specs=(hbm,) * 5,
        scratch_shapes=[*(pltpu.VMEM(x.shape, x.dtype) for x in outs), dma((8,)), dma((8,))],
        compiler_params=pltpu.CompilerParams(vmem_limit_bytes=60 * 1024 * 1024),
        name="results_to_hbm",
    )(*results)


def solution(mesh):
    row_bands, rows = P("dp", "mp", None), P("dp", "mp")
    return jax.shard_map(
        local,
        mesh=mesh,
        in_specs=(row_bands, row_bands, rows, row_bands, rows, row_bands, rows, row_bands, rows, P()),
        out_specs=(row_bands, rows, row_bands, rows, row_bands),
        check_vma=False,
    )
```

```python
import jax
import jax.numpy as jnp
from jax import lax
from jax.experimental import pallas as pl
from jax.experimental.pallas import tpu as pltpu
from jax.sharding import PartitionSpec as P

DECAY = 0.95
EPSILON = 1e-06
RING = 4
MESH = pl.DeviceIdType.MESH
F32, BF16 = jnp.float32, jnp.bfloat16


def dot(a, b, dims):
    return lax.dot_general(a, b, (dims, ((), ())), preferred_element_type=F32)


def kernel(
    plan_hbm, g_hbm, lc_hbm, ls_hbm, rc_hbm, rs_hbm, lrc_hbm, lrs_hbm, rrc_hbm, rrs_hbm,
    nl_hbm, nls_hbm, nr_hbm, nrs_hbm, up_hbm,
    plan_ref, g_ref, lc_ref, ls_ref, rc_ref, rs_ref, lrc_ref, lrs_ref, rrc_ref, rrs_ref,
    nl_ref, nls_ref, nr_ref, nrs_ref, up_ref,
    ya, lroot, lifted, acc_l, acc_r, acc_f, dirs, cols, codes, scol, grafted, st, first, second, landed,
    plan_s, info_v, info_s, sums_out, sums_in,
    ysend, yrecv, asend, arecv, psend, precv, isem, insem, outsem, word,
):
    owners = first.shape[0]
    height, width = g_ref.shape[1:]
    half = height // 2
    chunk = min(32, height)
    lanes = cols.shape[-1]
    groups = owners // (2 * RING)
    piece_rows = height // groups
    me, my_owner = lax.axis_index("mp"), lax.axis_index("dp")
    right, left = lax.rem(me + 1, RING), lax.rem(me + RING - 1, RING)

    halves = (pl.ds(0, half), pl.ds(half, half))

    def fetch(n, source, target):
        return pltpu.make_async_copy(source, target, insem.at[n])

    inputs = [
        fetch(n, *pair)
        for n, pair in enumerate(
            (
                (plan_hbm, plan_s), (g_hbm, g_ref), (ls_hbm, ls_ref), (lc_hbm, lc_ref), (rs_hbm, rs_ref),
                (rc_hbm, rc_ref), (lrs_hbm, lrs_ref), (rrs_hbm, rrs_ref), (lrc_hbm, lrc_ref), (rrc_hbm, rrc_ref),
                (plan_hbm, plan_ref),
            )
        )
    ]
    inputs[0].start()
    inputs[1].start()
    outputs = [
        pltpu.make_async_copy(source, target, outsem.at[n])
        for n, (source, target) in enumerate(
            (
                (nl_ref, nl_hbm), (nls_ref, nls_hbm), (nr_ref, nr_hbm), (nrs_ref, nrs_hbm),
                *((up_ref.at[s, rows], up_hbm.at[s, rows]) for rows in halves for s in range(2)),
            )
        )
    ]

    core, z = lax.rem(my_owner, 2), lax.rem(lax.div(my_owner, 2), groups)
    x = lax.div(my_owner, 2 * groups)

    def owner_at(x, z, core):
        return {"dp": (x * groups + z) * 2 + core}

    def along_z(*steps):
        return [owner_at(x, lax.rem(z + step, groups), core) for step in steps]

    beside_x = [owner_at(lax.rem(x + step, RING), z, core) for step in range(1, RING)]
    other_core = [owner_at(x, z, 1 - core)]
    ring = [{"mp": lax.rem(me + step, RING)} for step in range(1, RING)]
    below, above = (along_z(groups - 1), along_z(1)) if groups > 1 else ([], [])
    near = [*ring, *beside_x, *other_core, *below]
    barrier = pltpu.get_barrier_semaphore()
    for device in near:
        pl.semaphore_signal(barrier, inc=1, device_id=device, device_id_type=MESH)
    rounds, reach = [above], 1
    while reach < groups // 2:
        rounds.append(along_z(reach, groups - reach))
        reach *= 2
    rounds += [other_core, beside_x]
    rounds = [[]] * (word.shape[0] - len(rounds)) + rounds

    def tell(n):
        for device in rounds[n]:
            pl.semaphore_signal(word.at[n], inc=1, device_id=device, device_id_type=MESH)

    def hear(n):
        if rounds[n]:
            pl.semaphore_wait(word.at[n], len(rounds[n]))

    inputs[0].wait()
    moves = [lax.shift_right_logical(plan_s[0, 2 * my_owner + slot], 1) != my_owner for slot in range(2)]
    vacancy, present = jnp.where(moves[1], 1, 0), moves[0] | moves[1]
    slots = (vacancy, 1 - vacancy)

    def routing():
        inputs[10].wait()
        blocks = plan_ref.shape[1]
        plan = jnp.transpose(jnp.broadcast_to(plan_ref[...], (blocks, blocks)))
        block = lax.broadcasted_iota(jnp.int32, (blocks, blocks), 0)
        owner = lax.broadcasted_iota(jnp.int32, (blocks, blocks), 1)
        target, anchor = lax.shift_right_logical(plan, 1), lax.shift_right_logical(block, 1)
        arrives = (target != anchor) & (target == owner)
        info_v[0:1, :] = jnp.max(jnp.where(arrives, anchor, jnp.zeros_like(block)), axis=0, keepdims=True)
        pltpu.make_async_copy(info_v, info_s, isem).start()

    def over_rows(body):
        @pl.loop(0, height // chunk)
        def _(r):
            body(pl.ds(pl.multiple_of(r * chunk, chunk), chunk))

    def wide(column, columns=width):
        return jnp.concatenate([column] * (columns // lanes), axis=1) if columns > lanes else column[:, :columns]

    def stage(p):
        def body(rows):
            ya[p, 0, rows, :] = g_ref[slots[p], rows, :]

        over_rows(body)

    def scale_columns(n, ref):
        both = ref[...].astype(F32)
        pair = (both[0:1, :], both[1:2, :])
        for p in range(2):
            row = jnp.where(vacancy == p, pair[0], pair[1])
            cols[n, p] = jnp.transpose(jnp.broadcast_to(row, (lanes, height)))

    inputs[1].wait()
    stage(0)
    pl.semaphore_wait(barrier, len(near))

    def hop(a, kind):
        source, target, which, to = (
            (0, 1, 0, right), (0, 1, 1, right), (0, 2, 0, left), (0, 2, 1, left), (1, 3, 0, right), (2, 3, 1, left),
        )[kind]
        return pltpu.make_async_remote_copy(
            src_ref=ya.at[a, source, halves[which]],
            dst_ref=ya.at[a, target, halves[which]],
            send_sem=ysend.at[a, kind],
            recv_sem=yrecv.at[a, kind],
            device_id={"mp": to},
            device_id_type=MESH,
        )

    def start(a, *kinds):
        for kind in kinds:
            hop(a, kind).start()

    def arrived(a, *kinds):
        for kind in kinds:
            hop(a, kind).wait_recv()

    start(0, 0, 3, 1, 2)
    for copy in inputs[2:]:
        copy.start()

    deltas = (0, RING - 1, 1, 2)

    def columns(k):
        return pl.ds(pl.multiple_of(k * height, height), height)

    def piece(j):
        q = lax.div(j, 2)
        group = lax.rem(q, groups)
        tile = lax.rem(lax.div(q, groups) + group, RING)
        return lax.rem(j, 2), tile, pl.ds(pl.multiple_of(group * piece_rows, piece_rows), piece_rows)

    mine = piece(my_owner)

    def spread(side, tile):
        @pl.loop(0, groups)
        def _(step):
            group = lax.rem(lax.rem(lax.div(my_owner, 2), groups) + step, groups)
            peer = (lax.rem(tile + RING * groups - group, RING) * groups + group) * 2 + side
            source = st.at[side, tile, pl.ds(pl.multiple_of(group * piece_rows, piece_rows), piece_rows)]

            @pl.when(peer != my_owner)
            def _():
                pltpu.make_async_remote_copy(
                    src_ref=source,
                    dst_ref=first.at[my_owner],
                    send_sem=asend.at[0],
                    recv_sem=arecv.at[0],
                    device_id={"dp": peer},
                    device_id_type=MESH,
                ).start()

    def all_but_mine(sem):
        others = first.at[pl.ds(0, owners - 1)]
        pltpu.make_async_copy(others, others, sem).wait()

    def deliver_all():
        pltpu.make_async_copy(info_v, info_s, isem).wait()
        first[my_owner] = st[mine]
        all_but_mine(arecv.at[0])

        @pl.loop(0, owners)
        def _(d):
            second[d] = first[info_s[0, d]]

        @pl.loop(1, owners)
        def _(step):
            peer = lax.rem(my_owner + step, owners)
            pltpu.make_async_remote_copy(
                src_ref=second.at[peer],
                dst_ref=landed.at[mine],
                send_sem=asend.at[1],
                recv_sem=arecv.at[1],
                device_id={"dp": peer},
                device_id_type=MESH,
            ).start()

        landed[mine] = second[my_owner]

    def left_tile(p, rel):
        k = columns(lax.rem(me + deltas[rel], RING))
        tile = dot(ya[p, 0], ya[p, rel], ((1,), (1,)))
        old = lc_ref[slots[p], :, k].astype(F32) * wide(cols[0, p], height)
        m = DECAY * old + tile
        acc_l[p, :, k] = m
        if p == 0:
            st[0, rel] = m.astype(BF16)
            spread(0, rel)

    def band(p, rel):
        k = columns(lax.rem(me + deltas[rel], RING))
        both = jnp.concatenate([jnp.transpose(ya[p, rel, :, columns(me)]), lroot[p, :, k]], axis=0)

        @pl.loop(0, RING)
        def _(n):
            cs = columns(n)
            y = dot(both, ya[p, rel, :, cs], ((1,), (0,)))
            if rel == 0:
                acc_r[p, :, cs] = y[:height]
                acc_f[:, cs] = y[height:]
            else:
                acc_r[p, :, cs] += y[:height]
                acc_f[:, cs] += y[height:]

    def right_tiles(p):
        @pl.loop(0, RING)
        def _(n):
            cs = columns(n)
            m = DECAY * (rc_ref[slots[p], :, cs].astype(F32) * wide(cols[1, p], height)) + acc_r[p, :, cs]
            acc_r[p, :, cs] = m
            if p == 0:
                st[1, n] = m.astype(BF16)
                spread(1, n)

    def requantize(m):
        scale = (jnp.max(jnp.abs(m), axis=1, keepdims=True) + EPSILON).astype(BF16).astype(F32)
        return (m / scale).astype(BF16), jnp.broadcast_to(scale, (scale.shape[0], lanes))

    def finish(p):
        def body(rows):
            lifted[p, rows, :] = acc_f[rows, :].astype(BF16)
            for side, acc in enumerate((acc_l, acc_r)):
                codes[p, side, rows, :], scol[p, side, rows, :] = requantize(acc[p, rows, :])

        over_rows(body)

    def roots(p):
        def body(rows):
            lroot[p, rows, :] = (lrc_ref[slots[p], rows, :].astype(F32) * wide(cols[2, p, rows, :])).astype(BF16)
            ya[2 + p, 0, rows, :] = (rrc_ref[slots[p], rows, :].astype(F32) * wide(cols[3, p, rows, :])).astype(BF16)

        over_rows(body)

    def squares(x):
        total = jnp.zeros((8, lanes), F32)
        x = jnp.sum(jnp.reshape(x * x, (x.shape[0] // 8, 8, x.shape[1])), axis=0)
        for c in range(max(x.shape[1] // lanes, 1)):
            total = total + x[:, c * lanes : (c + 1) * lanes]
        return total

    def gradient_norm(p):
        sums_out[p] = jnp.zeros((16, lanes), F32)

        def body(rows):
            sums_out[p, 0:8, :] += squares(ya[p, 0, rows, :].astype(F32))

        over_rows(body)

    def direction(p, rel):
        k = columns(lax.rem(me + deltas[rel], RING))

        @pl.loop(0, RING)
        def _(n):
            cs = columns(n)
            d = dot(lifted[p, :, k], ya[2 + p, rel, :, cs], ((1,), (0,)))
            if rel == 0:
                dirs[p, :, cs] = d
            else:
                d = dirs[p, :, cs] + d
                dirs[p, :, cs] = d
            if rel == RING - 1:
                sums_out[p, 8:16, :] += squares(d)

    def share(p, step):
        return pltpu.make_async_remote_copy(
            src_ref=sums_out.at[p],
            dst_ref=sums_in.at[p, step - 1],
            send_sem=psend.at[p, step - 1],
            recv_sem=precv.at[p, step - 1],
            device_id={"mp": lax.rem(me + step, RING)},
            device_id_type=MESH,
        )

    def norms(p):
        for step in range(1, RING):
            share(p, step).start()

    def ratio(p):
        total = sums_out[p]
        for step in range(1, RING):
            share(p, step).wait_recv()
            total = total + sums_in[p, step - 1]
        grad_total = jnp.sum(total[0:8, :], keepdims=True)
        dir_total = jnp.sum(total[8:16, :], keepdims=True)
        return jnp.sqrt(grad_total + EPSILON) / jnp.sqrt(dir_total + EPSILON)

    def graft(p):
        r = ratio(p)
        for part in range(2):

            @pl.loop(0, half // chunk)
            def _(n):
                rows = pl.ds(pl.multiple_of(part * half + n * chunk, chunk), chunk)
                update = (dirs[p, rows, :] * r).astype(BF16)
                if p == 0:
                    grafted[rows, :] = update
                else:
                    up_ref[0, rows, :] = jnp.where(vacancy == 0, grafted[rows, :], update)
                    up_ref[1, rows, :] = jnp.where(vacancy == 0, update, grafted[rows, :])

            if p == 1:
                for copy in outputs[4 + 2 * part : 6 + 2 * part]:
                    copy.start()

    tell(0)
    stage(1)
    for n in range(2, 10):
        inputs[n].wait()
    for n, ref in enumerate((ls_ref, rs_ref, lrs_ref)):
        scale_columns(n, ref)
    hear(0)
    tell(1)
    scale_columns(3, rrs_ref)
    roots(0)
    arrived(0, 0, 3)
    start(0, 4, 5)
    hear(1)
    tell(2)
    routing()
    band(0, 0)
    hear(2)
    tell(3)
    gradient_norm(0)
    arrived(0, 1, 2)
    start(1, 0, 3, 1, 2)
    hear(3)
    tell(4)
    band(0, 1)
    band(0, 2)
    hear(4)
    left_tile(0, 0)
    left_tile(0, 1)
    left_tile(0, 2)
    roots(1)
    arrived(0, 4, 5)
    left_tile(0, 3)
    band(0, 3)
    right_tiles(0)
    finish(0)
    gradient_norm(1)
    left_tile(1, 0)
    band(1, 0)
    arrived(1, 0, 3)
    start(1, 4, 5)
    start(2, 0, 3, 1, 2)
    direction(0, 0)
    deliver_all()
    arrived(1, 1, 2)
    for rel in (1, 2):
        left_tile(1, rel)
        band(1, rel)
    arrived(1, 4, 5)
    left_tile(1, 3)
    band(1, 3)
    right_tiles(1)
    finish(1)
    arrived(2, 0, 3)
    start(2, 4, 5)
    start(3, 0, 3, 1, 2)
    direction(1, 0)
    arrived(2, 1, 2)
    direction(0, 1)
    direction(0, 2)
    arrived(2, 4, 5)
    direction(0, 3)
    norms(0)
    arrived(3, 0, 3)
    start(3, 4, 5)
    graft(0)

    all_but_mine(arecv.at[1])

    def arriving(rows):
        for side, out in enumerate((nl_ref, nr_ref)):
            m = [landed[side, t, rows, :].astype(F32) for t in range(RING)]
            top = jnp.maximum(jnp.maximum(jnp.abs(m[0]), jnp.abs(m[1])), jnp.maximum(jnp.abs(m[2]), jnp.abs(m[3])))
            scale = (jnp.max(top, axis=1, keepdims=True) + EPSILON).astype(BF16).astype(F32)
            for t in range(RING):
                cs = columns(lax.rem(me + deltas[t], RING)) if side == 0 else pl.ds(t * height, height)
                fresh = (m[t] / scale).astype(BF16)
                first_code = jnp.where(present, fresh, codes[0, side, rows, cs])
                other_code = codes[1, side, rows, cs]
                out[0, rows, cs] = jnp.where(vacancy == 0, first_code, other_code)
                out[1, rows, cs] = jnp.where(vacancy == 0, other_code, first_code)
            scol[0, side, rows, :] = jnp.where(
                present, jnp.broadcast_to(scale, (scale.shape[0], lanes)), scol[0, side, rows, :]
            )

    over_rows(arriving)
    for side, out in enumerate((nls_ref, nrs_ref)):
        pair = [jnp.transpose(scol[p, side])[0:1, :] for p in range(2)]
        upper = jnp.where(vacancy == 0, pair[0], pair[1])
        lower = jnp.where(vacancy == 0, pair[1], pair[0])
        out[...] = jnp.concatenate([upper, lower], axis=0).astype(BF16)
    for copy in outputs[:4]:
        copy.start()

    arrived(3, 1, 2)
    direction(1, 1)
    direction(1, 2)
    for a in range(3):
        for kind in range(6):
            hop(a, kind).wait_send()
    for phase in range(2):
        all_but_mine(asend.at[phase])
    arrived(3, 4, 5)
    direction(1, 3)
    norms(1)
    graft(1)

    for kind in range(6):
        hop(3, kind).wait_send()
    for p in range(2):
        for step in range(1, RING):
            share(p, step).wait_send()
    for copy in outputs:
        copy.wait()


def results_to_hbm(*refs):
    n = len(refs[:-2]) // 3
    insem, outsem = refs[-2:]
    parts = []
    for i in range(n):
        source, target, held = refs[i], refs[n + i], refs[2 * n + i]
        slices = [pl.ds(0, 1), pl.ds(1, 1)] if len(held.shape) == 3 else [pl.ds(0, held.shape[0])]
        for part in slices:
            m = len(parts)
            parts.append(
                (
                    pltpu.make_async_copy(source.at[part], held.at[part], insem.at[m]),
                    pltpu.make_async_copy(held.at[part], target.at[part], outsem.at[m]),
                )
            )
    for inward, _ in parts:
        inward.start()
    for inward, outward in parts:
        inward.wait()
        outward.start()
    for _, outward in parts:
        outward.wait()


def local(*args):
    *arrays, plan = args
    slots, height, width = arrays[0].shape
    owners = lax.axis_size("dp")
    blocks = plan.shape[0]
    lanes = 128
    piece_rows = height // (owners // (2 * RING))
    big = jax.ShapeDtypeStruct((slots, height, width), BF16)
    small = jax.ShapeDtypeStruct((slots, height), BF16)
    outs = (big, small, big, small, big)
    hbm = pl.BlockSpec(memory_space=pl.ANY)
    dma = pltpu.SemaphoreType.DMA
    held = [plan.reshape(1, blocks), *arrays]
    results = pl.pallas_call(
        kernel,
        out_shape=outs,
        in_specs=[hbm] * 10,
        out_specs=(hbm,) * 5,
        scratch_shapes=[
            *(pltpu.VMEM(x.shape, x.dtype) for x in (*held, *outs)),
            pltpu.VMEM((4, RING, height, width), BF16),
            pltpu.VMEM((2, height, width), BF16),
            pltpu.VMEM((2, height, width), BF16),
            pltpu.VMEM((2, height, width), F32),
            pltpu.VMEM((2, height, width), F32),
            pltpu.VMEM((height, width), F32),
            pltpu.VMEM((2, height, width), F32),
            pltpu.VMEM((4, 2, height, lanes), F32),
            pltpu.VMEM((2, 2, height, width), BF16),
            pltpu.VMEM((2, 2, height, lanes), F32),
            pltpu.VMEM((height, width), BF16),
            pltpu.VMEM((2, RING, height, height), BF16),
            pltpu.VMEM((owners, piece_rows, height), BF16),
            pltpu.VMEM((owners, piece_rows, height), BF16),
            pltpu.VMEM((2, RING, height, height), BF16),
            pltpu.SMEM((1, blocks), jnp.int32),
            pltpu.VMEM((8, blocks), jnp.int32),
            pltpu.SMEM((8, blocks), jnp.int32),
            pltpu.VMEM((2, 16, lanes), F32),
            pltpu.VMEM((2, RING - 1, 16, lanes), F32),
            dma((4, 6)),
            dma((4, 6)),
            dma((2,)),
            dma((2,)),
            dma((2, RING - 1)),
            dma((2, RING - 1)),
            dma,
            dma((11,)),
            dma((8,)),
            pltpu.SemaphoreType.REGULAR((5,)),
        ],
        compiler_params=pltpu.CompilerParams(
            collective_id=0, has_side_effects=True, vmem_limit_bytes=60 * 1024 * 1024
        ),
        name="shampoo_step",
    )(*held)
    return pl.pallas_call(
        results_to_hbm,
        out_shape=outs,
        in_specs=[hbm] * 5,
        out_specs=(hbm,) * 5,
        scratch_shapes=[*(pltpu.VMEM(x.shape, x.dtype) for x in outs), dma((8,)), dma((8,))],
        compiler_params=pltpu.CompilerParams(vmem_limit_bytes=60 * 1024 * 1024),
        name="results_to_hbm",
    )(*results)


def solution(mesh):
    row_bands, rows = P("dp", "mp", None), P("dp", "mp")
    return jax.shard_map(
        local,
        mesh=mesh,
        in_specs=(row_bands, row_bands, rows, row_bands, rows, row_bands, rows, row_bands, rows, P()),
        out_specs=(row_bands, rows, row_bands, rows, row_bands),
        check_vma=False,
    )
```

```python
import jax
import jax.numpy as jnp
from jax import lax
from jax.experimental import pallas as pl
from jax.experimental.pallas import tpu as pltpu
from jax.sharding import PartitionSpec as P

DECAY = 0.95
EPSILON = 1e-06
RING = 4
MESH = pl.DeviceIdType.MESH
F32, BF16 = jnp.float32, jnp.bfloat16


def dot(a, b, dims):
    return lax.dot_general(a, b, (dims, ((), ())), preferred_element_type=F32)


def graft_ratio(sums):
    grad_total = jnp.sum(sums[0:8, :], keepdims=True)
    dir_total = jnp.sum(sums[8:16, :], keepdims=True)
    return jnp.sqrt(grad_total + EPSILON) / jnp.sqrt(dir_total + EPSILON)


def kernel(
    plan_hbm, g_hbm, lc_hbm, ls_hbm, rc_hbm, rs_hbm, lrc_hbm, lrs_hbm, rrc_hbm, rrs_hbm,
    nl_hbm, nls_hbm, nr_hbm, nrs_hbm, dir_hbm, grafted_hbm, sums_hbm,
    plan_ref, g_ref, lc_ref, ls_ref, rc_ref, rs_ref, lrc_ref, lrs_ref, rrc_ref, rrs_ref,
    nl_ref, nls_ref, nr_ref, nrs_ref,
    ya, lroot, lifted, acc_l, acc_r, acc_f, dirs, cols, codes, scol, grafted, st, first, second, landed,
    plan_s, info_v, info_s, sums_out, sums_in,
    ysend, yrecv, asend, arecv, psend, precv, isem, insem, outsem, word,
):
    owners = first.shape[0]
    height, width = g_ref.shape[1:]
    half = height // 2
    chunk = min(32, height)
    lanes = cols.shape[-1]
    groups = owners // (2 * RING)
    piece_rows = height // groups
    me, my_owner = lax.axis_index("mp"), lax.axis_index("dp")
    right, left = lax.rem(me + 1, RING), lax.rem(me + RING - 1, RING)

    halves = (pl.ds(0, half), pl.ds(half, half))

    def fetch(n, source, target):
        return pltpu.make_async_copy(source, target, insem.at[n])

    inputs = [
        fetch(n, *pair)
        for n, pair in enumerate(
            (
                (plan_hbm, plan_s), (g_hbm, g_ref), (ls_hbm, ls_ref), (lc_hbm, lc_ref), (rs_hbm, rs_ref),
                (rc_hbm, rc_ref), (lrs_hbm, lrs_ref), (rrs_hbm, rrs_ref), (lrc_hbm, lrc_ref), (rrc_hbm, rrc_ref),
                (plan_hbm, plan_ref),
            )
        )
    ]
    inputs[0].start()
    inputs[1].start()
    outputs = [
        pltpu.make_async_copy(source, target, outsem.at[n])
        for n, (source, target) in enumerate(
            (
                (nl_ref, nl_hbm), (nls_ref, nls_hbm), (nr_ref, nr_hbm), (nrs_ref, nrs_hbm),
                (dirs.at[1], dir_hbm), (grafted, grafted_hbm),
                (sums_out.at[1], sums_hbm.at[0]), (sums_in.at[1], sums_hbm.at[pl.ds(1, RING - 1)]),
            )
        )
    ]

    core, z = lax.rem(my_owner, 2), lax.rem(lax.div(my_owner, 2), groups)
    x = lax.div(my_owner, 2 * groups)

    def owner_at(x, z, core):
        return {"dp": (x * groups + z) * 2 + core}

    def along_z(*steps):
        return [owner_at(x, lax.rem(z + step, groups), core) for step in steps]

    beside_x = [owner_at(lax.rem(x + step, RING), z, core) for step in range(1, RING)]
    other_core = [owner_at(x, z, 1 - core)]
    ring = [{"mp": lax.rem(me + step, RING)} for step in range(1, RING)]
    below, above = (along_z(groups - 1), along_z(1)) if groups > 1 else ([], [])
    near = [*ring, *beside_x, *other_core, *below]
    barrier = pltpu.get_barrier_semaphore()
    for device in near:
        pl.semaphore_signal(barrier, inc=1, device_id=device, device_id_type=MESH)
    rounds, reach = [above], 1
    while reach < groups // 2:
        rounds.append(along_z(reach, groups - reach))
        reach *= 2
    rounds += [other_core, beside_x]
    rounds = [[]] * (word.shape[0] - len(rounds)) + rounds

    def tell(n):
        for device in rounds[n]:
            pl.semaphore_signal(word.at[n], inc=1, device_id=device, device_id_type=MESH)

    def hear(n):
        if rounds[n]:
            pl.semaphore_wait(word.at[n], len(rounds[n]))

    inputs[0].wait()
    moves = [lax.shift_right_logical(plan_s[0, 2 * my_owner + slot], 1) != my_owner for slot in range(2)]
    vacancy, present = jnp.where(moves[1], 1, 0), moves[0] | moves[1]
    slots = (vacancy, 1 - vacancy)

    def routing():
        inputs[10].wait()
        blocks = plan_ref.shape[1]
        plan = jnp.transpose(jnp.broadcast_to(plan_ref[...], (blocks, blocks)))
        block = lax.broadcasted_iota(jnp.int32, (blocks, blocks), 0)
        owner = lax.broadcasted_iota(jnp.int32, (blocks, blocks), 1)
        target, anchor = lax.shift_right_logical(plan, 1), lax.shift_right_logical(block, 1)
        arrives = (target != anchor) & (target == owner)
        info_v[0:1, :] = jnp.max(jnp.where(arrives, anchor, jnp.zeros_like(block)), axis=0, keepdims=True)
        pltpu.make_async_copy(info_v, info_s, isem).start()

    def over_rows(body):
        @pl.loop(0, height // chunk)
        def _(r):
            body(pl.ds(pl.multiple_of(r * chunk, chunk), chunk))

    def wide(column, columns=width):
        return jnp.concatenate([column] * (columns // lanes), axis=1) if columns > lanes else column[:, :columns]

    def stage(p):
        def body(rows):
            ya[p, 0, rows, :] = g_ref[slots[p], rows, :]

        over_rows(body)

    def scale_columns(n, ref):
        both = ref[...].astype(F32)
        pair = (both[0:1, :], both[1:2, :])
        for p in range(2):
            row = jnp.where(vacancy == p, pair[0], pair[1])
            cols[n, p] = jnp.transpose(jnp.broadcast_to(row, (lanes, height)))

    inputs[1].wait()
    stage(0)
    pl.semaphore_wait(barrier, len(near))

    def hop(a, kind):
        source, target, which, to = (
            (0, 1, 0, right), (0, 1, 1, right), (0, 2, 0, left), (0, 2, 1, left), (1, 3, 0, right), (2, 3, 1, left),
        )[kind]
        return pltpu.make_async_remote_copy(
            src_ref=ya.at[a, source, halves[which]],
            dst_ref=ya.at[a, target, halves[which]],
            send_sem=ysend.at[a, kind],
            recv_sem=yrecv.at[a, kind],
            device_id={"mp": to},
            device_id_type=MESH,
        )

    def start(a, *kinds):
        for kind in kinds:
            hop(a, kind).start()

    def arrived(a, *kinds):
        for kind in kinds:
            hop(a, kind).wait_recv()

    start(0, 0, 3, 1, 2)
    for copy in inputs[2:]:
        copy.start()

    deltas = (0, RING - 1, 1, 2)

    def columns(k):
        return pl.ds(pl.multiple_of(k * height, height), height)

    def piece(j):
        q = lax.div(j, 2)
        group = lax.rem(q, groups)
        tile = lax.rem(lax.div(q, groups) + group, RING)
        return lax.rem(j, 2), tile, pl.ds(pl.multiple_of(group * piece_rows, piece_rows), piece_rows)

    mine = piece(my_owner)

    def spread(side, tile):
        @pl.loop(0, groups)
        def _(step):
            group = lax.rem(lax.rem(lax.div(my_owner, 2), groups) + step, groups)
            peer = (lax.rem(tile + RING * groups - group, RING) * groups + group) * 2 + side
            source = st.at[side, tile, pl.ds(pl.multiple_of(group * piece_rows, piece_rows), piece_rows)]

            @pl.when(peer != my_owner)
            def _():
                pltpu.make_async_remote_copy(
                    src_ref=source,
                    dst_ref=first.at[my_owner],
                    send_sem=asend.at[0],
                    recv_sem=arecv.at[0],
                    device_id={"dp": peer},
                    device_id_type=MESH,
                ).start()

    def all_but_mine(sem):
        others = first.at[pl.ds(0, owners - 1)]
        pltpu.make_async_copy(others, others, sem).wait()

    def deliver_all():
        pltpu.make_async_copy(info_v, info_s, isem).wait()
        first[my_owner] = st[mine]
        all_but_mine(arecv.at[0])

        @pl.loop(0, owners)
        def _(d):
            second[d] = first[info_s[0, d]]

        @pl.loop(1, owners)
        def _(step):
            peer = lax.rem(my_owner + step, owners)
            pltpu.make_async_remote_copy(
                src_ref=second.at[peer],
                dst_ref=landed.at[mine],
                send_sem=asend.at[1],
                recv_sem=arecv.at[1],
                device_id={"dp": peer},
                device_id_type=MESH,
            ).start()

        landed[mine] = second[my_owner]

    def left_tile(p, rel):
        k = columns(lax.rem(me + deltas[rel], RING))
        tile = dot(ya[p, 0], ya[p, rel], ((1,), (1,)))
        old = lc_ref[slots[p], :, k].astype(F32) * wide(cols[0, p], height)
        m = DECAY * old + tile
        acc_l[p, :, k] = m
        if p == 0:
            st[0, rel] = m.astype(BF16)
            spread(0, rel)

    def band(p, rel):
        k = columns(lax.rem(me + deltas[rel], RING))
        both = jnp.concatenate([jnp.transpose(ya[p, rel, :, columns(me)]), lroot[p, :, k]], axis=0)

        @pl.loop(0, RING)
        def _(n):
            cs = columns(n)
            y = dot(both, ya[p, rel, :, cs], ((1,), (0,)))
            if rel == 0:
                acc_r[p, :, cs] = y[:height]
                acc_f[:, cs] = y[height:]
            else:
                acc_r[p, :, cs] += y[:height]
                acc_f[:, cs] += y[height:]

    def right_tiles(p):
        @pl.loop(0, RING)
        def _(n):
            cs = columns(n)
            m = DECAY * (rc_ref[slots[p], :, cs].astype(F32) * wide(cols[1, p], height)) + acc_r[p, :, cs]
            acc_r[p, :, cs] = m
            if p == 0:
                st[1, n] = m.astype(BF16)
                spread(1, n)

    def requantize(m):
        scale = (jnp.max(jnp.abs(m), axis=1, keepdims=True) + EPSILON).astype(BF16).astype(F32)
        return (m / scale).astype(BF16), jnp.broadcast_to(scale, (scale.shape[0], lanes))

    def finish(p):
        def body(rows):
            lifted[p, rows, :] = acc_f[rows, :].astype(BF16)
            for side, acc in enumerate((acc_l, acc_r)):
                codes[p, side, rows, :], scol[p, side, rows, :] = requantize(acc[p, rows, :])

        over_rows(body)

    def roots(p):
        def body(rows):
            lroot[p, rows, :] = (lrc_ref[slots[p], rows, :].astype(F32) * wide(cols[2, p, rows, :])).astype(BF16)
            ya[2 + p, 0, rows, :] = (rrc_ref[slots[p], rows, :].astype(F32) * wide(cols[3, p, rows, :])).astype(BF16)

        over_rows(body)

    def squares(x):
        total = jnp.zeros((8, lanes), F32)
        x = jnp.sum(jnp.reshape(x * x, (x.shape[0] // 8, 8, x.shape[1])), axis=0)
        for c in range(max(x.shape[1] // lanes, 1)):
            total = total + x[:, c * lanes : (c + 1) * lanes]
        return total

    def gradient_norm(p):
        sums_out[p] = jnp.zeros((16, lanes), F32)

        def body(rows):
            sums_out[p, 0:8, :] += squares(ya[p, 0, rows, :].astype(F32))

        over_rows(body)

    def direction(p, rel):
        k = columns(lax.rem(me + deltas[rel], RING))

        @pl.loop(0, RING)
        def _(n):
            cs = columns(n)
            d = dot(lifted[p, :, k], ya[2 + p, rel, :, cs], ((1,), (0,)))
            if rel == 0:
                dirs[p, :, cs] = d
            else:
                d = dirs[p, :, cs] + d
                dirs[p, :, cs] = d
            if rel == RING - 1:
                sums_out[p, 8:16, :] += squares(d)

    def share(p, step):
        return pltpu.make_async_remote_copy(
            src_ref=sums_out.at[p],
            dst_ref=sums_in.at[p, step - 1],
            send_sem=psend.at[p, step - 1],
            recv_sem=precv.at[p, step - 1],
            device_id={"mp": lax.rem(me + step, RING)},
            device_id_type=MESH,
        )

    def norms(p):
        for step in range(1, RING):
            share(p, step).start()

    def graft_leaving():
        total = sums_out[0]
        for step in range(1, RING):
            share(0, step).wait_recv()
            total = total + sums_in[0, step - 1]
        r = graft_ratio(total)

        def body(rows):
            grafted[rows, :] = (dirs[0, rows, :] * r).astype(BF16)

        over_rows(body)

    tell(0)
    stage(1)
    for n in range(2, 10):
        inputs[n].wait()
    for n, ref in enumerate((ls_ref, rs_ref, lrs_ref)):
        scale_columns(n, ref)
    hear(0)
    tell(1)
    scale_columns(3, rrs_ref)
    roots(0)
    arrived(0, 0, 3)
    start(0, 4, 5)
    hear(1)
    tell(2)
    routing()
    band(0, 0)
    hear(2)
    tell(3)
    gradient_norm(0)
    arrived(0, 1, 2)
    start(1, 0, 3, 1, 2)
    hear(3)
    tell(4)
    band(0, 1)
    band(0, 2)
    hear(4)
    left_tile(0, 0)
    left_tile(0, 1)
    left_tile(0, 2)
    roots(1)
    arrived(0, 4, 5)
    left_tile(0, 3)
    band(0, 3)
    right_tiles(0)
    finish(0)
    gradient_norm(1)
    left_tile(1, 0)
    band(1, 0)
    arrived(1, 0, 3)
    start(1, 4, 5)
    start(2, 0, 3, 1, 2)
    direction(0, 0)
    deliver_all()
    arrived(1, 1, 2)
    for rel in (1, 2):
        left_tile(1, rel)
        band(1, rel)
    arrived(1, 4, 5)
    left_tile(1, 3)
    band(1, 3)
    right_tiles(1)
    finish(1)
    arrived(2, 0, 3)
    start(2, 4, 5)
    start(3, 0, 3, 1, 2)
    direction(1, 0)
    arrived(2, 1, 2)
    direction(0, 1)
    direction(0, 2)
    arrived(2, 4, 5)
    direction(0, 3)
    norms(0)
    arrived(3, 0, 3)
    start(3, 4, 5)
    graft_leaving()
    outputs[5].start()

    all_but_mine(arecv.at[1])

    def arriving(rows):
        for side, out in enumerate((nl_ref, nr_ref)):
            m = [landed[side, t, rows, :].astype(F32) for t in range(RING)]
            top = jnp.maximum(jnp.maximum(jnp.abs(m[0]), jnp.abs(m[1])), jnp.maximum(jnp.abs(m[2]), jnp.abs(m[3])))
            scale = (jnp.max(top, axis=1, keepdims=True) + EPSILON).astype(BF16).astype(F32)
            for t in range(RING):
                cs = columns(lax.rem(me + deltas[t], RING)) if side == 0 else pl.ds(t * height, height)
                fresh = (m[t] / scale).astype(BF16)
                first_code = jnp.where(present, fresh, codes[0, side, rows, cs])
                other_code = codes[1, side, rows, cs]
                out[0, rows, cs] = jnp.where(vacancy == 0, first_code, other_code)
                out[1, rows, cs] = jnp.where(vacancy == 0, other_code, first_code)
            scol[0, side, rows, :] = jnp.where(
                present, jnp.broadcast_to(scale, (scale.shape[0], lanes)), scol[0, side, rows, :]
            )

    over_rows(arriving)
    for side, out in enumerate((nls_ref, nrs_ref)):
        pair = [jnp.transpose(scol[p, side])[0:1, :] for p in range(2)]
        upper = jnp.where(vacancy == 0, pair[0], pair[1])
        lower = jnp.where(vacancy == 0, pair[1], pair[0])
        out[...] = jnp.concatenate([upper, lower], axis=0).astype(BF16)
    for copy in outputs[:4]:
        copy.start()

    arrived(3, 1, 2)
    direction(1, 1)
    direction(1, 2)
    for a in range(3):
        for kind in range(6):
            hop(a, kind).wait_send()
    for phase in range(2):
        all_but_mine(asend.at[phase])
    arrived(3, 4, 5)
    direction(1, 3)
    norms(1)
    outputs[4].start()
    outputs[6].start()
    for step in range(1, RING):
        share(1, step).wait_recv()
    outputs[7].start()

    for kind in range(6):
        hop(3, kind).wait_send()
    for p in range(2):
        for step in range(1, RING):
            share(p, step).wait_send()
    for copy in outputs:
        copy.wait()


def results_to_hbm(
    plan_hbm, nl_in, nls_in, nr_in, nrs_in, dir_in, grafted_in, sums_in,
    nl_out, nls_out, nr_out, nrs_out, up_out,
    plan_s, nl, nls, nr, nrs, direction, grafted, sums, up,
    insem, outsem,
):
    height = direction.shape[0]
    half, chunk = height // 2, min(32, height // 2)
    halves = (pl.ds(0, half), pl.ds(half, half))
    inward = [
        pltpu.make_async_copy(source, target, insem.at[n])
        for n, (source, target) in enumerate(
            (
                (plan_hbm, plan_s), (sums_in, sums),
                (dir_in.at[halves[0]], direction.at[halves[0]]), (grafted_in, grafted),
                (dir_in.at[halves[1]], direction.at[halves[1]]),
                (nl_in.at[0], nl.at[0]), (nl_in.at[1], nl.at[1]), (nr_in.at[0], nr.at[0]), (nr_in.at[1], nr.at[1]),
                (nls_in, nls), (nrs_in, nrs),
            )
        )
    ]
    outward = [
        pltpu.make_async_copy(source, target, outsem.at[n])
        for n, (source, target) in enumerate(
            (
                *((up.at[slot, rows], up_out.at[slot, rows]) for rows in halves for slot in range(2)),
                (nl.at[0], nl_out.at[0]), (nl.at[1], nl_out.at[1]), (nr.at[0], nr_out.at[0]), (nr.at[1], nr_out.at[1]),
                (nls, nls_out), (nrs, nrs_out),
            )
        )
    ]
    for copy in inward:
        copy.start()
    inward[0].wait()
    my_owner = lax.axis_index("dp")
    first_is_0 = lax.shift_right_logical(plan_s[0, 2 * my_owner + 1], 1) == my_owner
    inward[1].wait()
    ratio = graft_ratio((sums[0] + sums[1]) + (sums[2] + sums[3]))

    def graft(part):
        @pl.loop(0, half // chunk)
        def _(n):
            rows = pl.ds(pl.multiple_of(part * half + n * chunk, chunk), chunk)
            update, leaving = (direction[rows, :] * ratio).astype(BF16), grafted[rows, :]
            up[0, rows, :] = jnp.where(first_is_0, leaving, update)
            up[1, rows, :] = jnp.where(first_is_0, update, leaving)

    def on(first, last):
        for n in range(first, last):
            inward[n + 1].wait()
            outward[n].start()

    inward[2].wait()
    inward[3].wait()
    graft(0)
    outward[0].start()
    outward[1].start()
    on(4, 6)
    inward[4].wait()
    graft(1)
    outward[2].start()
    outward[3].start()
    on(6, 10)
    for copy in outward:
        copy.wait()


def local(*args):
    *arrays, plan = args
    slots, height, width = arrays[0].shape
    owners = lax.axis_size("dp")
    blocks = plan.shape[0]
    lanes = 128
    piece_rows = height // (owners // (2 * RING))
    big = jax.ShapeDtypeStruct((slots, height, width), BF16)
    small = jax.ShapeDtypeStruct((slots, height), BF16)
    outs = (big, small, big, small, big)
    between = (
        *outs[:4],
        jax.ShapeDtypeStruct((height, width), F32),
        jax.ShapeDtypeStruct((height, width), BF16),
        jax.ShapeDtypeStruct((RING, 16, lanes), F32),
    )
    hbm = pl.BlockSpec(memory_space=pl.ANY)
    dma = pltpu.SemaphoreType.DMA
    held = [plan.reshape(1, blocks), *arrays]
    results = pl.pallas_call(
        kernel,
        out_shape=between,
        in_specs=[hbm] * 10,
        out_specs=(hbm,) * 7,
        scratch_shapes=[
            *(pltpu.VMEM(x.shape, x.dtype) for x in (*held, *outs[:4])),
            pltpu.VMEM((4, RING, height, width), BF16),
            pltpu.VMEM((2, height, width), BF16),
            pltpu.VMEM((2, height, width), BF16),
            pltpu.VMEM((2, height, width), F32),
            pltpu.VMEM((2, height, width), F32),
            pltpu.VMEM((height, width), F32),
            pltpu.VMEM((2, height, width), F32),
            pltpu.VMEM((4, 2, height, lanes), F32),
            pltpu.VMEM((2, 2, height, width), BF16),
            pltpu.VMEM((2, 2, height, lanes), F32),
            pltpu.VMEM((height, width), BF16),
            pltpu.VMEM((2, RING, height, height), BF16),
            pltpu.VMEM((owners, piece_rows, height), BF16),
            pltpu.VMEM((owners, piece_rows, height), BF16),
            pltpu.VMEM((2, RING, height, height), BF16),
            pltpu.SMEM((1, blocks), jnp.int32),
            pltpu.VMEM((8, blocks), jnp.int32),
            pltpu.SMEM((8, blocks), jnp.int32),
            pltpu.VMEM((2, 16, lanes), F32),
            pltpu.VMEM((2, RING - 1, 16, lanes), F32),
            dma((4, 6)),
            dma((4, 6)),
            dma((2,)),
            dma((2,)),
            dma((2, RING - 1)),
            dma((2, RING - 1)),
            dma,
            dma((11,)),
            dma((8,)),
            pltpu.SemaphoreType.REGULAR((5,)),
        ],
        compiler_params=pltpu.CompilerParams(
            collective_id=0, has_side_effects=True, vmem_limit_bytes=60 * 1024 * 1024
        ),
        name="shampoo_step",
    )(*held)
    return pl.pallas_call(
        results_to_hbm,
        out_shape=outs,
        in_specs=[hbm] * 8,
        out_specs=(hbm,) * 5,
        scratch_shapes=[
            pltpu.SMEM((1, blocks), jnp.int32),
            *(pltpu.VMEM(x.shape, x.dtype) for x in (*between, big)),
            dma((11,)),
            dma((10,)),
        ],
        compiler_params=pltpu.CompilerParams(vmem_limit_bytes=60 * 1024 * 1024),
        name="results_to_hbm",
    )(held[0], *results)


def solution(mesh):
    row_bands, rows = P("dp", "mp", None), P("dp", "mp")
    return jax.shard_map(
        local,
        mesh=mesh,
        in_specs=(row_bands, row_bands, rows, row_bands, rows, row_bands, rows, row_bands, rows, P()),
        out_specs=(row_bands, rows, row_bands, rows, row_bands),
        check_vma=False,
    )
```

```python
import jax
import jax.numpy as jnp
from jax import lax
from jax.experimental import pallas as pl
from jax.experimental.pallas import tpu as pltpu
from jax.sharding import PartitionSpec as P

DECAY = 0.95
EPSILON = 1e-06
RING = 4
MESH = pl.DeviceIdType.MESH
F32, BF16 = jnp.float32, jnp.bfloat16


def dot(a, b, dims):
    return lax.dot_general(a, b, (dims, ((), ())), preferred_element_type=F32)


def graft_ratio(sums):
    grad_total = jnp.sum(sums[0:8, :], keepdims=True)
    dir_total = jnp.sum(sums[8:16, :], keepdims=True)
    return jnp.sqrt(grad_total + EPSILON) / jnp.sqrt(dir_total + EPSILON)


def kernel(
    plan_hbm, g_hbm, lc_hbm, ls_hbm, rc_hbm, rs_hbm, lrc_hbm, lrs_hbm, rrc_hbm, rrs_hbm,
    nl_hbm, nls_hbm, nr_hbm, nrs_hbm, dir_hbm, grafted_hbm, sums_hbm,
    plan_ref, g_ref, lc_ref, ls_ref, rc_ref, rs_ref, lrc_ref, lrs_ref, rrc_ref, rrs_ref,
    nl_ref, nls_ref, nr_ref, nrs_ref,
    ya, lroot, lifted, acc_l, acc_r, acc_f, dirs, cols, codes, scol, grafted, st, first, second, landed,
    plan_s, info_v, info_s, sums_out, sums_in,
    ysend, yrecv, asend, arecv, psend, precv, isem, insem, outsem, word,
):
    owners = first.shape[0]
    height, width = g_ref.shape[1:]
    half = height // 2
    chunk = min(32, height)
    lanes = cols.shape[-1]
    groups = owners // (2 * RING)
    piece_rows = height // groups
    me, my_owner = lax.axis_index("mp"), lax.axis_index("dp")
    right, left = lax.rem(me + 1, RING), lax.rem(me + RING - 1, RING)

    halves = (pl.ds(0, half), pl.ds(half, half))

    def fetch(n, source, target):
        return pltpu.make_async_copy(source, target, insem.at[n])

    inputs = [
        fetch(n, *pair)
        for n, pair in enumerate(
            (
                (plan_hbm, plan_s), (g_hbm, g_ref), (ls_hbm, ls_ref), (lc_hbm, lc_ref), (rs_hbm, rs_ref),
                (rc_hbm, rc_ref), (lrs_hbm, lrs_ref), (rrs_hbm, rrs_ref), (lrc_hbm, lrc_ref), (rrc_hbm, rrc_ref),
                (plan_hbm, plan_ref),
            )
        )
    ]
    inputs[0].start()
    inputs[1].start()
    outputs = [
        pltpu.make_async_copy(source, target, outsem.at[n])
        for n, (source, target) in enumerate(
            (
                (nl_ref, nl_hbm), (nls_ref, nls_hbm), (nr_ref, nr_hbm), (nrs_ref, nrs_hbm),
                (dirs.at[1], dir_hbm), (grafted, grafted_hbm),
                (sums_out.at[1], sums_hbm.at[0]), (sums_in.at[1], sums_hbm.at[pl.ds(1, RING - 1)]),
            )
        )
    ]

    core, z = lax.rem(my_owner, 2), lax.rem(lax.div(my_owner, 2), groups)
    x = lax.div(my_owner, 2 * groups)

    def owner_at(x, z, core):
        return {"dp": (x * groups + z) * 2 + core}

    def along_z(*steps):
        return [owner_at(x, lax.rem(z + step, groups), core) for step in steps]

    beside_x = [owner_at(lax.rem(x + step, RING), z, core) for step in range(1, RING)]
    other_core = [owner_at(x, z, 1 - core)]
    ring = [{"mp": lax.rem(me + step, RING)} for step in range(1, RING)]
    near = [*ring, *beside_x, *other_core]
    barrier = pltpu.get_barrier_semaphore()

    def signal(semaphore, device):
        pl.semaphore_signal(semaphore, inc=1, device_id=device, device_id_type=MESH)

    for device in near:
        signal(barrier, device)
    near_count = len(near)
    lowest, highest = z == 0, z == groups - 1
    if groups > 2:
        [below], [above] = along_z(groups - 1), along_z(1)
        near_count = near_count + jnp.where(lowest, 0, jnp.where(highest, 2, 1))

        @pl.when(z < groups - 1)
        def _():
            signal(barrier, above)

        @pl.when(lowest)
        def _():
            signal(barrier, below)

    rounds, reach = [[]], 1
    while reach < groups // 2:
        rounds.append(along_z(reach, groups - reach))
        reach *= 2
    rounds += [other_core, beside_x]
    rounds = [[]] * (word.shape[0] - len(rounds)) + rounds

    def tell(n):
        for device in rounds[n]:
            signal(word.at[n], device)
        if n == 0 and groups > 2:

            @pl.when(z > 0)
            def _():
                signal(word.at[n], below)

            @pl.when(highest)
            def _():
                signal(word.at[n], above)

    def hear(n):
        if rounds[n]:
            pl.semaphore_wait(word.at[n], len(rounds[n]))
        if n == 0 and groups > 2:

            @pl.when(z < groups - 1)
            def _():
                pl.semaphore_wait(word.at[n], jnp.where(lowest, 2, 1))

    inputs[0].wait()
    moves = [lax.shift_right_logical(plan_s[0, 2 * my_owner + slot], 1) != my_owner for slot in range(2)]
    vacancy, present = jnp.where(moves[1], 1, 0), moves[0] | moves[1]
    slots = (vacancy, 1 - vacancy)

    def routing():
        inputs[10].wait()
        blocks = plan_ref.shape[1]
        plan = jnp.transpose(jnp.broadcast_to(plan_ref[...], (blocks, blocks)))
        block = lax.broadcasted_iota(jnp.int32, (blocks, blocks), 0)
        owner = lax.broadcasted_iota(jnp.int32, (blocks, blocks), 1)
        target, anchor = lax.shift_right_logical(plan, 1), lax.shift_right_logical(block, 1)
        arrives = (target != anchor) & (target == owner)
        info_v[0:1, :] = jnp.max(jnp.where(arrives, anchor, jnp.zeros_like(block)), axis=0, keepdims=True)
        pltpu.make_async_copy(info_v, info_s, isem).start()

    def over_rows(body):
        @pl.loop(0, height // chunk)
        def _(r):
            body(pl.ds(pl.multiple_of(r * chunk, chunk), chunk))

    def wide(column, columns=width):
        return jnp.concatenate([column] * (columns // lanes), axis=1) if columns > lanes else column[:, :columns]

    def stage(p):
        def body(rows):
            ya[p, 0, rows, :] = g_ref[slots[p], rows, :]

        over_rows(body)

    def scale_columns(n, ref):
        both = ref[...].astype(F32)
        pair = (both[0:1, :], both[1:2, :])
        for p in range(2):
            row = jnp.where(vacancy == p, pair[0], pair[1])
            cols[n, p] = jnp.transpose(jnp.broadcast_to(row, (lanes, height)))

    inputs[1].wait()
    stage(0)
    pl.semaphore_wait(barrier, near_count)

    def hop(a, kind):
        source, target, which, to = (
            (0, 1, 0, right), (0, 1, 1, right), (0, 2, 0, left), (0, 2, 1, left), (1, 3, 0, right), (2, 3, 1, left),
        )[kind]
        return pltpu.make_async_remote_copy(
            src_ref=ya.at[a, source, halves[which]],
            dst_ref=ya.at[a, target, halves[which]],
            send_sem=ysend.at[a, kind],
            recv_sem=yrecv.at[a, kind],
            device_id={"mp": to},
            device_id_type=MESH,
        )

    def start(a, *kinds):
        for kind in kinds:
            hop(a, kind).start()

    def arrived(a, *kinds):
        for kind in kinds:
            hop(a, kind).wait_recv()

    start(0, 0, 3, 1, 2)
    for copy in inputs[2:]:
        copy.start()

    deltas = (0, RING - 1, 1, 2)

    def columns(k):
        return pl.ds(pl.multiple_of(k * height, height), height)

    def piece(j):
        q = lax.div(j, 2)
        group = lax.rem(q, groups)
        tile = lax.rem(lax.div(q, groups) + group, RING)
        return lax.rem(j, 2), tile, pl.ds(pl.multiple_of(group * piece_rows, piece_rows), piece_rows)

    mine = piece(my_owner)

    def spread(side, tile):
        @pl.loop(0, groups)
        def _(step):
            group = lax.rem(lax.rem(lax.div(my_owner, 2), groups) + step, groups)
            peer = (lax.rem(tile + RING * groups - group, RING) * groups + group) * 2 + side
            source = st.at[side, tile, pl.ds(pl.multiple_of(group * piece_rows, piece_rows), piece_rows)]

            @pl.when(peer != my_owner)
            def _():
                pltpu.make_async_remote_copy(
                    src_ref=source,
                    dst_ref=first.at[my_owner],
                    send_sem=asend.at[0],
                    recv_sem=arecv.at[0],
                    device_id={"dp": peer},
                    device_id_type=MESH,
                ).start()

    def all_but_mine(sem):
        others = first.at[pl.ds(0, owners - 1)]
        pltpu.make_async_copy(others, others, sem).wait()

    def deliver_all():
        pltpu.make_async_copy(info_v, info_s, isem).wait()
        first[my_owner] = st[mine]
        all_but_mine(arecv.at[0])

        @pl.loop(0, owners)
        def _(d):
            second[d] = first[info_s[0, d]]

        @pl.loop(1, owners)
        def _(step):
            peer = lax.rem(my_owner + step, owners)
            pltpu.make_async_remote_copy(
                src_ref=second.at[peer],
                dst_ref=landed.at[mine],
                send_sem=asend.at[1],
                recv_sem=arecv.at[1],
                device_id={"dp": peer},
                device_id_type=MESH,
            ).start()

        landed[mine] = second[my_owner]

    def left_tile(p, rel):
        k = columns(lax.rem(me + deltas[rel], RING))
        tile = dot(ya[p, 0], ya[p, rel], ((1,), (1,)))
        old = lc_ref[slots[p], :, k].astype(F32) * wide(cols[0, p], height)
        m = DECAY * old + tile
        acc_l[p, :, k] = m
        if p == 0:
            st[0, rel] = m.astype(BF16)
            spread(0, rel)

    def band(p, rel):
        k = columns(lax.rem(me + deltas[rel], RING))
        both = jnp.concatenate([jnp.transpose(ya[p, rel, :, columns(me)]), lroot[p, :, k]], axis=0)

        @pl.loop(0, RING)
        def _(n):
            cs = columns(n)
            y = dot(both, ya[p, rel, :, cs], ((1,), (0,)))
            if rel == 0:
                acc_r[p, :, cs] = y[:height]
                acc_f[:, cs] = y[height:]
            else:
                acc_r[p, :, cs] += y[:height]
                acc_f[:, cs] += y[height:]

    def right_tiles(p):
        @pl.loop(0, RING)
        def _(n):
            cs = columns(n)
            m = DECAY * (rc_ref[slots[p], :, cs].astype(F32) * wide(cols[1, p], height)) + acc_r[p, :, cs]
            acc_r[p, :, cs] = m
            if p == 0:
                st[1, n] = m.astype(BF16)
                spread(1, n)

    def requantize(m):
        scale = (jnp.max(jnp.abs(m), axis=1, keepdims=True) + EPSILON).astype(BF16).astype(F32)
        return (m / scale).astype(BF16), jnp.broadcast_to(scale, (scale.shape[0], lanes))

    def finish(p):
        def body(rows):
            lifted[p, rows, :] = acc_f[rows, :].astype(BF16)
            for side, acc in enumerate((acc_l, acc_r)):
                codes[p, side, rows, :], scol[p, side, rows, :] = requantize(acc[p, rows, :])

        over_rows(body)

    def roots(p):
        def body(rows):
            lroot[p, rows, :] = (lrc_ref[slots[p], rows, :].astype(F32) * wide(cols[2, p, rows, :])).astype(BF16)
            ya[2 + p, 0, rows, :] = (rrc_ref[slots[p], rows, :].astype(F32) * wide(cols[3, p, rows, :])).astype(BF16)

        over_rows(body)

    def squares(x):
        total = jnp.zeros((8, lanes), F32)
        x = jnp.sum(jnp.reshape(x * x, (x.shape[0] // 8, 8, x.shape[1])), axis=0)
        for c in range(max(x.shape[1] // lanes, 1)):
            total = total + x[:, c * lanes : (c + 1) * lanes]
        return total

    def gradient_norm(p):
        sums_out[p] = jnp.zeros((16, lanes), F32)

        def body(rows):
            sums_out[p, 0:8, :] += squares(ya[p, 0, rows, :].astype(F32))

        over_rows(body)

    def direction(p, rel):
        k = columns(lax.rem(me + deltas[rel], RING))

        @pl.loop(0, RING)
        def _(n):
            cs = columns(n)
            d = dot(lifted[p, :, k], ya[2 + p, rel, :, cs], ((1,), (0,)))
            if rel == 0:
                dirs[p, :, cs] = d
            else:
                d = dirs[p, :, cs] + d
                dirs[p, :, cs] = d
            if rel == RING - 1:
                sums_out[p, 8:16, :] += squares(d)

    def share(p, step):
        return pltpu.make_async_remote_copy(
            src_ref=sums_out.at[p],
            dst_ref=sums_in.at[p, step - 1],
            send_sem=psend.at[p, step - 1],
            recv_sem=precv.at[p, step - 1],
            device_id={"mp": lax.rem(me + step, RING)},
            device_id_type=MESH,
        )

    def norms(p):
        for step in range(1, RING):
            share(p, step).start()

    def graft_leaving():
        total = sums_out[0]
        for step in range(1, RING):
            share(0, step).wait_recv()
            total = total + sums_in[0, step - 1]
        r = graft_ratio(total)

        def body(rows):
            grafted[rows, :] = (dirs[0, rows, :] * r).astype(BF16)

        over_rows(body)

    tell(0)
    stage(1)
    for n in range(2, 10):
        inputs[n].wait()
    hear(0)
    tell(1)
    for n, ref in enumerate((ls_ref, rs_ref, lrs_ref, rrs_ref)):
        scale_columns(n, ref)
    hear(1)
    tell(2)
    roots(0)
    hear(2)
    tell(3)
    arrived(0, 0, 3)
    start(0, 4, 5)
    hear(3)
    tell(4)
    routing()
    band(0, 0)
    gradient_norm(0)
    arrived(0, 1, 2)
    start(1, 0, 3, 1, 2)
    hear(4)
    left_tile(0, 0)
    left_tile(0, 1)
    left_tile(0, 2)
    band(0, 1)
    band(0, 2)
    roots(1)
    arrived(0, 4, 5)
    left_tile(0, 3)
    band(0, 3)
    right_tiles(0)
    arrived(1, 0, 3)
    start(1, 4, 5)
    start(2, 0, 3, 1, 2)
    finish(0)
    gradient_norm(1)
    left_tile(1, 0)
    band(1, 0)
    direction(0, 0)
    deliver_all()
    arrived(1, 1, 2)
    for rel in (1, 2):
        left_tile(1, rel)
        band(1, rel)
    arrived(1, 4, 5)
    left_tile(1, 3)
    band(1, 3)
    right_tiles(1)
    finish(1)
    arrived(2, 0, 3)
    start(2, 4, 5)
    start(3, 0, 3, 1, 2)
    direction(1, 0)
    arrived(2, 1, 2)
    direction(0, 1)
    direction(0, 2)
    arrived(2, 4, 5)
    direction(0, 3)
    norms(0)
    arrived(3, 0, 3)
    start(3, 4, 5)
    graft_leaving()
    outputs[5].start()

    all_but_mine(arecv.at[1])

    def arriving(rows):
        for side, out in enumerate((nl_ref, nr_ref)):
            m = [landed[side, t, rows, :].astype(F32) for t in range(RING)]
            top = jnp.maximum(jnp.maximum(jnp.abs(m[0]), jnp.abs(m[1])), jnp.maximum(jnp.abs(m[2]), jnp.abs(m[3])))
            scale = (jnp.max(top, axis=1, keepdims=True) + EPSILON).astype(BF16).astype(F32)
            for t in range(RING):
                cs = columns(lax.rem(me + deltas[t], RING)) if side == 0 else pl.ds(t * height, height)
                fresh = (m[t] / scale).astype(BF16)
                first_code = jnp.where(present, fresh, codes[0, side, rows, cs])
                other_code = codes[1, side, rows, cs]
                out[0, rows, cs] = jnp.where(vacancy == 0, first_code, other_code)
                out[1, rows, cs] = jnp.where(vacancy == 0, other_code, first_code)
            scol[0, side, rows, :] = jnp.where(
                present, jnp.broadcast_to(scale, (scale.shape[0], lanes)), scol[0, side, rows, :]
            )

    over_rows(arriving)
    for side, out in enumerate((nls_ref, nrs_ref)):
        pair = [jnp.transpose(scol[p, side])[0:1, :] for p in range(2)]
        upper = jnp.where(vacancy == 0, pair[0], pair[1])
        lower = jnp.where(vacancy == 0, pair[1], pair[0])
        out[...] = jnp.concatenate([upper, lower], axis=0).astype(BF16)
    for copy in outputs[:4]:
        copy.start()

    arrived(3, 1, 2)
    direction(1, 1)
    direction(1, 2)
    for a in range(3):
        for kind in range(6):
            hop(a, kind).wait_send()
    for phase in range(2):
        all_but_mine(asend.at[phase])
    arrived(3, 4, 5)
    direction(1, 3)
    norms(1)
    outputs[4].start()
    outputs[6].start()
    for step in range(1, RING):
        share(1, step).wait_recv()
    outputs[7].start()

    for kind in range(6):
        hop(3, kind).wait_send()
    for p in range(2):
        for step in range(1, RING):
            share(p, step).wait_send()
    for copy in outputs:
        copy.wait()


def results_to_hbm(
    plan_hbm, nl_in, nls_in, nr_in, nrs_in, dir_in, grafted_in, sums_in,
    nl_out, nls_out, nr_out, nrs_out, up_out,
    plan_s, nl, nls, nr, nrs, direction, grafted, sums, up,
    insem, outsem,
):
    height = direction.shape[0]
    half, chunk = height // 2, min(32, height // 2)
    halves = (pl.ds(0, half), pl.ds(half, half))
    inward = [
        pltpu.make_async_copy(source, target, insem.at[n])
        for n, (source, target) in enumerate(
            (
                (plan_hbm, plan_s), (sums_in, sums),
                (dir_in.at[halves[0]], direction.at[halves[0]]), (grafted_in, grafted),
                (dir_in.at[halves[1]], direction.at[halves[1]]),
                (nl_in.at[0], nl.at[0]), (nl_in.at[1], nl.at[1]), (nr_in.at[0], nr.at[0]), (nr_in.at[1], nr.at[1]),
                (nls_in, nls), (nrs_in, nrs),
            )
        )
    ]
    outward = [
        pltpu.make_async_copy(source, target, outsem.at[n])
        for n, (source, target) in enumerate(
            (
                *((up.at[slot, rows], up_out.at[slot, rows]) for rows in halves for slot in range(2)),
                (nl.at[0], nl_out.at[0]), (nl.at[1], nl_out.at[1]), (nr.at[0], nr_out.at[0]), (nr.at[1], nr_out.at[1]),
                (nls, nls_out), (nrs, nrs_out),
            )
        )
    ]
    for copy in inward:
        copy.start()
    inward[0].wait()
    my_owner = lax.axis_index("dp")
    first_is_0 = lax.shift_right_logical(plan_s[0, 2 * my_owner + 1], 1) == my_owner
    inward[1].wait()
    ratio = graft_ratio((sums[0] + sums[1]) + (sums[2] + sums[3]))

    def graft(part):
        @pl.loop(0, half // chunk)
        def _(n):
            rows = pl.ds(pl.multiple_of(part * half + n * chunk, chunk), chunk)
            update, leaving = (direction[rows, :] * ratio).astype(BF16), grafted[rows, :]
            up[0, rows, :] = jnp.where(first_is_0, leaving, update)
            up[1, rows, :] = jnp.where(first_is_0, update, leaving)

    def on(first, last):
        for n in range(first, last):
            inward[n + 1].wait()
            outward[n].start()

    inward[2].wait()
    inward[3].wait()
    graft(0)
    outward[0].start()
    outward[1].start()
    on(4, 6)
    inward[4].wait()
    graft(1)
    outward[2].start()
    outward[3].start()
    on(6, 10)
    for copy in outward:
        copy.wait()


def local(*args):
    *arrays, plan = args
    slots, height, width = arrays[0].shape
    owners = lax.axis_size("dp")
    blocks = plan.shape[0]
    lanes = 128
    piece_rows = height // (owners // (2 * RING))
    big = jax.ShapeDtypeStruct((slots, height, width), BF16)
    small = jax.ShapeDtypeStruct((slots, height), BF16)
    outs = (big, small, big, small, big)
    between = (
        *outs[:4],
        jax.ShapeDtypeStruct((height, width), F32),
        jax.ShapeDtypeStruct((height, width), BF16),
        jax.ShapeDtypeStruct((RING, 16, lanes), F32),
    )
    hbm = pl.BlockSpec(memory_space=pl.ANY)
    dma = pltpu.SemaphoreType.DMA
    held = [plan.reshape(1, blocks), *arrays]
    results = pl.pallas_call(
        kernel,
        out_shape=between,
        in_specs=[hbm] * 10,
        out_specs=(hbm,) * 7,
        scratch_shapes=[
            *(pltpu.VMEM(x.shape, x.dtype) for x in (*held, *outs[:4])),
            pltpu.VMEM((4, RING, height, width), BF16),
            pltpu.VMEM((2, height, width), BF16),
            pltpu.VMEM((2, height, width), BF16),
            pltpu.VMEM((2, height, width), F32),
            pltpu.VMEM((2, height, width), F32),
            pltpu.VMEM((height, width), F32),
            pltpu.VMEM((2, height, width), F32),
            pltpu.VMEM((4, 2, height, lanes), F32),
            pltpu.VMEM((2, 2, height, width), BF16),
            pltpu.VMEM((2, 2, height, lanes), F32),
            pltpu.VMEM((height, width), BF16),
            pltpu.VMEM((2, RING, height, height), BF16),
            pltpu.VMEM((owners, piece_rows, height), BF16),
            pltpu.VMEM((owners, piece_rows, height), BF16),
            pltpu.VMEM((2, RING, height, height), BF16),
            pltpu.SMEM((1, blocks), jnp.int32),
            pltpu.VMEM((8, blocks), jnp.int32),
            pltpu.SMEM((8, blocks), jnp.int32),
            pltpu.VMEM((2, 16, lanes), F32),
            pltpu.VMEM((2, RING - 1, 16, lanes), F32),
            dma((4, 6)),
            dma((4, 6)),
            dma((2,)),
            dma((2,)),
            dma((2, RING - 1)),
            dma((2, RING - 1)),
            dma,
            dma((11,)),
            dma((8,)),
            pltpu.SemaphoreType.REGULAR((5,)),
        ],
        compiler_params=pltpu.CompilerParams(
            collective_id=0, has_side_effects=True, vmem_limit_bytes=60 * 1024 * 1024
        ),
        name="shampoo_step",
    )(*held)
    return pl.pallas_call(
        results_to_hbm,
        out_shape=outs,
        in_specs=[hbm] * 8,
        out_specs=(hbm,) * 5,
        scratch_shapes=[
            pltpu.SMEM((1, blocks), jnp.int32),
            *(pltpu.VMEM(x.shape, x.dtype) for x in (*between, big)),
            dma((11,)),
            dma((10,)),
        ],
        compiler_params=pltpu.CompilerParams(vmem_limit_bytes=60 * 1024 * 1024),
        name="results_to_hbm",
    )(held[0], *results)


def solution(mesh):
    row_bands, rows = P("dp", "mp", None), P("dp", "mp")
    return jax.shard_map(
        local,
        mesh=mesh,
        in_specs=(row_bands, row_bands, rows, row_bands, rows, row_bands, rows, row_bands, rows, P()),
        out_specs=(row_bands, rows, row_bands, rows, row_bands),
        check_vma=False,
    )
```
